128 devices in a mesh: group: 8 (over z, x_hi), tensor: 16 (over x_lo, y, core).
Axes of the slice: x: 4 (x_hi: 2, x_lo: 2; x = x_hi * 2 + x_lo), y: 4, z: 4, core: 2. Of those that a mesh axis runs over, the one named last changes fastest.
Arguments:
- frozen_base_matrix: bfloat16 [5120, 25600], P(None, 'tensor'), may hold values from -0.078125 to 0.078125
- master_a: float32 [64, 16, 320], P(None, 'tensor', 'group'), may hold values from -0.03125 to 0.03125
- moment1_a: float32 [64, 16, 320], P(None, 'tensor', 'group'), may hold values from -120 to 120
- moment2_a: float32 [64, 16, 320], P(None, 'tensor', 'group'), may hold values from 16 to 500
- master_b: float32 [64, 16, 1600], P(None, 'tensor', 'group'), may hold values from -1.2 to 1.2
- moment1_b: float32 [64, 16, 1600], P(None, 'tensor', 'group'), may hold values from -1.2 to 1.2
- moment2_b: float32 [64, 16, 1600], P(None, 'tensor', 'group'), may hold values from 0.002 to 0.06
- learner_token_inputs: bfloat16 [4096, 5120], P('group', 'tensor'), may hold values from -6 to 6
- learner_output_cotangents: bfloat16 [4096, 25600], P('group', 'tensor'), may hold values from -0.29882812 to 0.29882812
- rollout_inputs: bfloat16 [4096, 5120], P(('group', 'tensor')), may hold values from -6 to 6
Outputs:
- rollout_out: bfloat16 [4096, 25600], P('group', 'tensor')
- master_a_next: float32 [64, 16, 320], P(None, 'tensor', 'group')
- moment1_a_next: float32 [64, 16, 320], P(None, 'tensor', 'group')
- moment2_a_next: float32 [64, 16, 320], P(None, 'tensor', 'group')
- master_b_next: float32 [64, 16, 1600], P(None, 'tensor', 'group')
- moment1_b_next: float32 [64, 16, 1600], P(None, 'tensor', 'group')
- moment2_b_next: float32 [64, 16, 1600], P(None, 'tensor', 'group')
The draws below stay inside these ranges and needn't reach their ends.
All inputs are finite; a program needn't handle non-finite values.
Results may differ from the reference program's by a relative error of at most 0.006.
Values may be sent and summed in bfloat16 or wider, within the bound.
A program may use at most 128 MiB of HBM per device.

```python
import math
import jax
import jax.numpy as jnp

D = 5120
FF = 25600
R = 64
LEARN_TOKENS = 4096
ROLL_TOKENS = 4096
N_TENSOR = 16


def shard_levels(key, dims, shards, smallest, largest):
    gain = 1.0
    for axis_at, shards_of in shards:
        draws = jax.random.uniform(jax.random.fold_in(jax.random.fold_in(key, 6), axis_at), (shards_of,), jnp.float32, smallest / len(shards), largest / len(shards))
        gain = gain * jnp.repeat(jnp.exp(draws), dims[axis_at] // shards_of).reshape((-1,) + (1,) * (len(dims) - 1 - axis_at))
    return gain


def normal_values(own_key, shape, deviation, most, shards=(), held_as=jnp.bfloat16):
    drawn = deviation * jax.random.normal(own_key, shape, jnp.float32)
    if shards:
        drawn = drawn * shard_levels(own_key, shape, shards, -0.22, 0.18)
    return jnp.clip(drawn, -most, most).astype(held_as)


def setup_inputs(seed: int = 0) -> dict:
    keys = jax.random.split(jax.random.key(seed), 11)
    return {
        "frozen_base_matrix": normal_values(keys[0], (D, FF), D ** -0.5, 0.078125, ((1, 16),)),
        "master_a": normal_values(keys[1], (R, N_TENSOR, D // N_TENSOR), (8 * D) ** -0.5, 0.03125, ((1, 16), (2, 8)), jnp.float32),
        "moment1_a": normal_values(keys[2], (R, N_TENSOR, D // N_TENSOR), 20.0, 120.0, ((1, 16), (2, 8)), jnp.float32),
        "moment2_a": jnp.clip(jnp.exp(math.log(500.0) - 3.4420194 * jax.random.uniform(keys[3], (R, N_TENSOR, D // N_TENSOR), jnp.float32) ** shard_levels(keys[3], (R, N_TENSOR, D // N_TENSOR), ((1, 16), (2, 8)), -0.2, 0.2)), 16.0, 500.0),
        "master_b": normal_values(keys[4], (R, N_TENSOR, FF // N_TENSOR), 0.2, 1.2, ((1, 16), (2, 8)), jnp.float32),
        "moment1_b": normal_values(keys[5], (R, N_TENSOR, FF // N_TENSOR), 0.2, 1.2, ((1, 16), (2, 8)), jnp.float32),
        "moment2_b": jnp.clip(jnp.exp(math.log(0.06) - 3.4011973 * jax.random.uniform(keys[6], (R, N_TENSOR, FF // N_TENSOR), jnp.float32) ** shard_levels(keys[6], (R, N_TENSOR, FF // N_TENSOR), ((1, 16), (2, 8)), -0.2, 0.2)), 0.002, 0.06),
        "learner_token_inputs": normal_values(keys[7], (LEARN_TOKENS, D), 1.0, 6.0, ((0, 8), (1, 16))),
        "learner_output_cotangents": normal_values(keys[8], (LEARN_TOKENS, FF), 0.05, 0.29882812, ((0, 8), (1, 16))),
        "rollout_inputs": normal_values(keys[9], (ROLL_TOKENS, D), 1.0, 6.0, ((0, 128),)),
    }


beta_one = 0.9
beta_two = 0.999
learn_rate = 0.001
adam_eps = 1e-08
adapter_scale = 2.0
fix_one = 0.9999734386011124
fix_two = 0.0952078528862904

def adam_step(master, first, second, grad):
    first_next = beta_one * first + (1.0 - beta_one) * grad
    second_next = beta_two * second + (1.0 - beta_two) * grad * grad
    master_next = master - learn_rate * (first_next / fix_one) / (jnp.sqrt(second_next / fix_two) + adam_eps)
    return (master_next, first_next, second_next)

def reference(frozen_base_matrix, master_a, moment1_a, moment2_a, master_b, moment1_b, moment2_b, learner_token_inputs, learner_output_cotangents, rollout_inputs):
    old_a = master_a.reshape(R, D).astype(jnp.bfloat16)
    old_b = master_b.reshape(R, FF).astype(jnp.bfloat16)
    hidden_lowrank = jnp.dot(learner_token_inputs, old_a.T, preferred_element_type=jnp.float32).astype(jnp.bfloat16)
    backward_lowrank = jnp.dot(learner_output_cotangents, old_b.T, preferred_element_type=jnp.float32).astype(jnp.bfloat16)
    down_factor_gradient = adapter_scale * jnp.dot(backward_lowrank.T, learner_token_inputs, preferred_element_type=jnp.float32)
    up_factor_gradient = adapter_scale * jnp.dot(hidden_lowrank.T, learner_output_cotangents, preferred_element_type=jnp.float32)
    master_a_next, moment1_a_next, moment2_a_next = adam_step(master_a, moment1_a, moment2_a, down_factor_gradient.reshape(master_a.shape))
    master_b_next, moment1_b_next, moment2_b_next = adam_step(master_b, moment1_b, moment2_b, up_factor_gradient.reshape(master_b.shape))
    new_a = master_a_next.reshape(R, D).astype(jnp.bfloat16)
    new_b = master_b_next.reshape(R, FF).astype(jnp.bfloat16)
    adapter_rank = jnp.dot(new_a.T, new_b, preferred_element_type=jnp.float32)
    merged_weight_matrix = (frozen_base_matrix.astype(jnp.float32) + adapter_scale * adapter_rank).astype(jnp.bfloat16)
    rollout_out = jnp.dot(rollout_inputs, merged_weight_matrix, preferred_element_type=jnp.float32).astype(jnp.bfloat16)
    return (rollout_out, master_a_next, moment1_a_next, moment2_a_next, master_b_next, moment1_b_next, moment2_b_next)
```

```python
import functools

import jax
import jax.numpy as jnp
from jax import lax
from jax.experimental import pallas as pl
from jax.experimental.pallas import tpu as pltpu
from jax.sharding import PartitionSpec as P

beta_one = 0.9
beta_two = 0.999
learn_rate = 0.001
adam_eps = 1e-08
adapter_scale = 2.0
fix_one = 0.9999734386011124
fix_two = 0.0952078528862904

MESH = pl.DeviceIdType.MESH
BF = jnp.bfloat16
F32 = jnp.float32

D, HID, TOK, COLS, ROWS = 5120, 1600, 512, 320, 32
SHARE_A, SHARE_B, RANK = 40, 200, 64
NT, NG = 16, 8

TENSOR_STEPS = sorted(
    ((dx, dy, dc) for dx in range(2) for dy in range(4) for dc in range(2) if (dx, dy, dc) != (0, 0, 0)),
    key=lambda s: -(s[0] + min(s[1], 4 - s[1]) + 0.1 * s[2]),
)
GROUP_STEPS = sorted(
    ((dz, dx) for dz in range(4) for dx in range(2) if (dz, dx) != (0, 0)),
    key=lambda s: -(min(s[0], 4 - s[0]) + 2 * s[1]),
)


def dot(left, right, left_dim, right_dim):
    return lax.dot_general(
        left, right, (((left_dim,), (right_dim,)), ((), ())), preferred_element_type=F32
    )


def aligned(index, size):
    return pl.ds(pl.multiple_of(index * size, size), size)


def kernel(
    base_hbm, ma_hbm, m1a_hbm, m2a_hbm, mb_hbm, m1b_hbm, m2b_hbm, xt_hbm, cot_hbm, xr_hbm,
    out_hbm, ma_out, m1a_out, m2a_out, mb_out, m1b_out, m2b_out,
    base, xt, cot, xall, acc, out_v, a_in, b_in, pad, msg0, got0, msg0b, mom_a, mom_b,
    old_a, old_b, part, got1, low, own2, grad_b, grad_a, msg3, got3, stats, msg4, got4, b_rows, b_left, b_right,
    a_left, a_right, part5, got5, own5, xa, b_out,
    loc, s0, r0, s0b, r0b, s1, r1, s2, r2, s3, r3, s4, r4, s5, r5, s6, r6, sx, rx, sc, rc,
):
    g = lax.axis_index("group")
    t = lax.axis_index("tensor")
    z, far = g // 2, lax.rem(g, 2)
    xl, y, core = t // 8, lax.rem(t // 2, 4), lax.rem(t, 2)

    def tensor_at(dx, dy, dc):
        return lax.rem(xl + dx, 2) * 8 + lax.rem(y + dy, 4) * 2 + lax.rem(core + dc, 2)

    def group_at(dz, dx):
        return lax.rem(z + dz, 4) * 2 + lax.rem(far + dx, 2)

    tensor_peers = [tensor_at(*s) for s in TENSOR_STEPS]
    group_peers = [group_at(*s) for s in GROUP_STEPS]

    def remote(src, dst, ssem, rsem, k, gg, tt):
        copy = pltpu.make_async_remote_copy(
            src_ref=src, dst_ref=dst, send_sem=ssem.at[k], recv_sem=rsem.at[k],
            device_id=(gg, tt), device_id_type=MESH,
        )
        copy.start()
        return copy

    sent = []

    def load(src, dst, k):
        copy = pltpu.make_async_copy(src, dst, loc.at[k])
        copy.start()
        return copy

    loads_b = [load(ref, b_in.at[i], i) for i, ref in enumerate((mb_hbm, m1b_hbm, m2b_hbm))]
    loads_a = [load(ref, a_in.at[i], 3 + i) for i, ref in enumerate((ma_hbm, m1a_hbm, m2a_hbm))]
    mine = aligned(t, ROWS)
    load_x = load(xr_hbm, xall.at[mine], 6)
    load_cot = load(cot_hbm, cot, 7)
    load_xt = load(xt_hbm, xt, 8)
    load_base = load(base_hbm, base, 9)

    bar = pltpu.get_barrier_semaphore()
    for gg in group_peers:
        pl.semaphore_signal(bar, inc=1, device_id=(gg, t), device_id_type=MESH)
    for tt in tensor_peers:
        pl.semaphore_signal(bar, inc=1, device_id=(g, tt), device_id_type=MESH)

    pad[...] = jnp.zeros_like(pad)
    for copy in loads_b + loads_a:
        copy.wait()
    pad[0, 0:SHARE_A, 0:RANK] = a_in[0]
    factor_a = pad[0].T[0:RANK, 0:SHARE_A]
    msg0[...] = jnp.zeros_like(msg0)
    msg0[:, 0:SHARE_B] = b_in[0, :, 0, :].astype(BF)
    msg0[:, SHARE_B:SHARE_B + SHARE_A] = factor_a.astype(BF)
    got0[g] = msg0[...]
    pl.semaphore_wait(bar, len(group_peers) + len(tensor_peers))

    copies0 = [remote(msg0, got0.at[g], s0, r0, k, gg, t) for k, gg in enumerate(group_peers)]

    x_next, y_up, y_down, sibling = tensor_at(1, 0, 0), tensor_at(0, 1, 0), tensor_at(0, 3, 0), tensor_at(0, 0, 1)
    half = D // 2
    low_half, high_half, all_of = pl.ds(0, half), pl.ds(half, half), pl.ds(0, D)

    def send_x(owner, columns, k, to):
        where = xall.at[aligned(owner, ROWS), columns]
        return remote(where, where, sx, rx, k, g, to)

    def share_x(owner, k):
        where = xall.at[aligned(owner, ROWS)]
        return remote(where, where, sc, rc, k, g, sibling)

    load_x.wait()
    step1 = [send_x(t, all_of, 0, x_next), send_x(t, all_of, 1, y_up), send_x(t, all_of, 2, y_down)]
    shared = [share_x(t, 0)]

    msg0b[...] = jnp.zeros_like(msg0b)
    msg0b[0, :, 0:RANK] = a_in[1]
    msg0b[0, :, RANK:2 * RANK] = a_in[0]
    msg0b[1, :, RANK:2 * RANK] = a_in[2]
    rows_a = aligned(g, SHARE_A)
    mom_a[:, rows_a, :] = msg0b[...]
    copies0b = [
        remote(msg0b, mom_a.at[:, rows_a, :], s0b, r0b, k, gg, t) for k, gg in enumerate(group_peers)
    ]

    mom_b[...] = jnp.zeros_like(mom_b)
    for i in range(3):
        pad[1, 0:RANK, 0:128] = b_in[i, :, 0, 0:128]
        pad[2, 0:RANK, 0:SHARE_B - 128] = b_in[i, :, 0, 128:SHARE_B]
        mom_b[i, 0:128, :] = pad[1].T
        mom_b[i, 128:256, :] = pad[2].T
    a_left[...] = jnp.zeros_like(a_left)
    a_right[...] = jnp.zeros_like(a_right)
    grad_b[HID:HID + 8, :] = jnp.zeros((8, 128), F32)

    for copy in copies0:
        copy.wait_recv()
    for j in range(NG):
        old_b[:, j * SHARE_B:(j + 1) * SHARE_B] = got0[j, :, 0:SHARE_B]
        old_a[:, j * SHARE_A:(j + 1) * SHARE_A] = got0[j, :, SHARE_B:SHARE_B + SHARE_A]
    load_cot.wait()
    load_xt.wait()
    hidden = dot(old_a[...], xt[...], 1, 0)
    back = dot(old_b[...], cot[...], 1, 0)
    for h in range(2):
        part[h, 0:RANK, :] = hidden[:, h * 256:(h + 1) * 256].astype(BF)
        part[h, RANK:, :] = back[:, h * 256:(h + 1) * 256].astype(BF)
    copies1 = [
        remote(part.at[lax.rem(tt, 2), aligned(tt // 2, 16)], got1.at[k], s1, r1, k, g, tt)
        for k, tt in enumerate(tensor_peers)
    ]

    for copy in step1:
        copy.wait_recv()
    of_x, of_up, of_down = x_next, y_up, y_down
    step2 = [
        send_x(of_up, low_half, 3, x_next),
        send_x(of_down, low_half, 4, x_next),
        send_x(of_x, high_half, 5, y_up),
        send_x(of_x, high_half, 6, y_down),
        send_x(of_down, low_half, 7, y_up),
        send_x(of_up, high_half, 8, y_down),
    ]
    shared += [share_x(of_x, 1), share_x(of_up, 2), share_x(of_down, 3)]

    for copy in copies1:
        copy.wait_recv()
    my_half, my_rows = lax.rem(t, 2), aligned(t // 2, 16)
    total = part[my_half, my_rows, :].astype(F32)
    for k in range(NT - 1):
        total = total + got1[k].astype(F32)
    own2[...] = total.astype(BF)
    low[my_half, my_rows, :] = own2[...]
    copies2 = [
        remote(own2, low.at[my_half, my_rows], s2, r2, k, g, tt) for k, tt in enumerate(tensor_peers)
    ]
    for copy in copies2:
        copy.wait_recv()

    low0, low1 = low[0], low[1]
    grad_a[...] = dot(xt[:, 0:256], low0, 1, 1) + dot(xt[:, 256:512], low1, 1, 1)

    def grad_rows(i, carry):
        rows = aligned(i, 400)
        grad_b[rows, :] = dot(cot[rows, 0:256], low0, 1, 1) + dot(cot[rows, 256:512], low1, 1, 1)
        return carry

    lax.fori_loop(0, HID // 400, grad_rows, 0)
    lanes = lax.broadcasted_iota(jnp.int32, (COLS, 128), 1)
    left = lanes < RANK

    def message3(j):
        rows = pl.ds(pl.multiple_of(j * SHARE_B, 8), 208)
        return jnp.where(left[0:208], grad_b[rows, :], grad_a[0:208, :]).astype(BF)

    rest = grad_a[208:COLS, :].astype(BF)
    copies3 = []
    for k, gg in enumerate(group_peers):
        msg3[k, 0:208, :] = message3(gg)
        msg3[k, 208:COLS, :] = rest
        copies3.append(remote(msg3.at[k], got3.at[g], s3, r3, k, gg, t))
    got3[g, 0:208, :] = message3(g)
    got3[g, 208:COLS, :] = rest

    for copy in step2:
        copy.wait_recv()
    across = tensor_at(0, 2, 0)
    quarter = D // 4
    step3 = [
        send_x(across, low_half, 9, x_next),
        send_x(tensor_at(1, 1, 0), pl.ds(2 * quarter, quarter), 10, y_down),
        send_x(tensor_at(1, 3, 0), pl.ds(3 * quarter, quarter), 11, y_up),
    ]
    shared += [share_x(across, 4), share_x(tensor_at(1, 1, 0), 5), share_x(tensor_at(1, 3, 0), 6)]

    def base_rows(h, first, last):
        tokens = aligned(h, 256)

        def body(i, carry):
            rows = aligned(i, 800)
            acc[h, rows, :] = dot(base[rows, :], xall[tokens, :], 1, 1)
            return carry

        lax.fori_loop(first, last, body, 0)

    load_base.wait()
    for k in (0, 2, 3, 4):
        shared[k].wait_recv()
    base_rows(xl, 0, 2)

    for copy in copies0b:
        copy.wait_recv()
    for copy in copies3:
        copy.wait_recv()
    grad = got3[0].astype(F32)
    for j in range(1, NG):
        grad = grad + got3[j].astype(F32)
    grad = adapter_scale * grad
    master = jnp.where(left, mom_b[0], mom_a[0])
    first = jnp.where(left, mom_b[1], pltpu.roll(mom_a[0], RANK, 1))
    second = jnp.where(left, mom_b[2], mom_a[1])
    first_next = beta_one * first + (1.0 - beta_one) * grad
    second_next = beta_two * second + (1.0 - beta_two) * grad * grad
    master_next = master - learn_rate * (first_next / fix_one) / (
        jnp.sqrt(second_next / fix_two) + adam_eps
    )
    stats[0] = master_next
    stats[1] = first_next
    stats[2] = second_next
    factors = master_next.astype(BF).astype(F32)
    only_a = jnp.where(left, 0.0, factors)
    place = pl.ds(pl.multiple_of(core * RANK, RANK), COLS)
    a_right[place, :] = only_a.astype(BF)
    a_left[place, :] = pltpu.roll(only_a, RANK, 1).astype(BF)
    msg4[...] = jnp.where(left[0:208], factors[0:208], 0.0).astype(BF)
    got4[g] = msg4[...]
    copies4 = [remote(msg4, got4.at[g], s4, r4, k, gg, t) for k, gg in enumerate(group_peers)]

    for copy in step3:
        copy.wait_recv()
    shared.append(share_x(tensor_at(1, 2, 0), 7))
    for k in (1, 5, 6, 7):
        shared[k].wait_recv()
    window = pl.ds(pl.multiple_of((t // 2) * 640 + core * 256, 128), 384)
    part5[...] = (
        dot(xall[0:256, window], a_left[...], 1, 0) + dot(xall[256:512, window], a_right[...], 1, 0)
    ).astype(BF)
    copies5 = [
        remote(part5.at[aligned(tt, 16)], got5.at[k], s5, r5, k, g, tt)
        for k, tt in enumerate(tensor_peers)
    ]

    base_rows(1 - xl, 0, 1)

    for copy in copies5:
        copy.wait_recv()
    mine5 = aligned(t, 16)
    total = part5[mine5, :].astype(F32)
    for k in range(NT - 1):
        total = total + got5[k].astype(F32)
    own5[...] = (adapter_scale * total).astype(BF)
    xa[mine5, :] = own5[...]
    copies6 = [remote(own5, xa.at[mine5], s6, r6, k, g, tt) for k, tt in enumerate(tensor_peers)]

    base_rows(1 - xl, 1, 2)

    rows_out = aligned(g, SHARE_A)
    for i in range(3):
        a_in[i] = pltpu.roll(stats[i, rows_out, :], RANK, 1)[:, 0:RANK]
        b_out[i, :, 0, 0:128] = stats[i, 0:128, :].T[0:RANK]
        b_out[i, :, 0, 128:SHARE_B] = stats[i, 128:256, :].T[0:RANK, 0:SHARE_B - 128]
    stores = [load(a_in.at[i], ref, 10 + i) for i, ref in enumerate((ma_out, m1a_out, m2a_out))]
    stores += [load(b_out.at[i], ref, 13 + i) for i, ref in enumerate((mb_out, m1b_out, m2b_out))]

    for copy in copies4:
        copy.wait_recv()
    for j in range(NG):
        b_rows[j * SHARE_B:(j + 1) * SHARE_B, :] = got4[j, 0:SHARE_B, :].astype(F32)
    b_left[...] = b_rows[...].astype(BF)
    b_right[...] = pltpu.roll(b_rows[...], RANK, 1).astype(BF)

    for copy in copies6:
        copy.wait_recv()
    for i in range(5):
        rows = pl.ds(320 * i, 320)
        out_v[rows, 0:256] = (acc[0, rows, :] + dot(b_left[rows, :], xa[...], 1, 1)).astype(BF)
        out_v[rows, 256:512] = (acc[1, rows, :] + dot(b_right[rows, :], xa[...], 1, 1)).astype(BF)
        stores.append(load(out_v.at[rows], out_hbm.at[rows], 16 + i))

    for group in (copies0, step1, shared, copies0b, copies1, step2, copies2, copies3, step3, copies4, copies5, copies6):
        for copy in group:
            copy.wait_send()
    for copy in stores:
        copy.wait()


def shards(
    frozen_base_matrix, master_a, moment1_a, moment2_a, master_b, moment1_b, moment2_b,
    learner_token_inputs, learner_output_cotangents, rollout_inputs,
):
    state_a = [ref.reshape(RANK, SHARE_A).T for ref in (master_a, moment1_a, moment2_a)]
    dma = pltpu.SemaphoreType.DMA
    vmem = pltpu.VMEM
    any_space = pl.BlockSpec(memory_space=pl.ANY)
    shape = jax.ShapeDtypeStruct
    results = pl.pallas_call(
        kernel,
        out_shape=[shape((HID, TOK), BF)]
        + [shape((SHARE_A, RANK), F32)] * 3
        + [shape((RANK, 1, SHARE_B), F32)] * 3,
        in_specs=[any_space] * 10,
        out_specs=[any_space] * 7,
        scratch_shapes=[
            vmem((HID, D), BF),
            vmem((COLS, TOK), BF),
            vmem((HID, TOK), BF),
            vmem((TOK, D), BF),
            vmem((2, HID, 256), F32),
            vmem((HID, TOK), BF),
            vmem((3, SHARE_A, RANK), F32),
            vmem((3, RANK, 1, SHARE_B), F32),
            vmem((3, 128, 128), F32),
            vmem((RANK, 256), BF),
            vmem((NG, RANK, 256), BF),
            vmem((2, SHARE_A, 128), F32),
            vmem((2, COLS, 128), F32),
            vmem((3, COLS, 128), F32),
            vmem((RANK, COLS), BF),
            vmem((RANK, HID), BF),
            vmem((2, 128, 256), BF),
            vmem((NT - 1, 16, 256), BF),
            vmem((2, 128, 256), BF),
            vmem((16, 256), BF),
            vmem((HID + 8, 128), F32),
            vmem((COLS, 128), F32),
            vmem((NG - 1, COLS, 128), BF),
            vmem((NG, COLS, 128), BF),
            vmem((3, COLS, 128), F32),
            vmem((208, 128), BF),
            vmem((NG, 208, 128), BF),
            vmem((HID, 128), F32),
            vmem((HID, 128), BF),
            vmem((HID, 128), BF),
            vmem((384, 128), BF),
            vmem((384, 128), BF),
            vmem((256, 128), BF),
            vmem((NT - 1, 16, 128), BF),
            vmem((16, 128), BF),
            vmem((256, 128), BF),
            vmem((3, RANK, 1, SHARE_B), F32),
            dma((24,)),
        ]
        + [dma((n,)) for n in (7, 7, 7, 7, 15, 15, 15, 15, 7, 7, 7, 7, 15, 15, 15, 15, 12, 12, 8, 8)],
        compiler_params=pltpu.CompilerParams(
            collective_id=0, has_side_effects=True, vmem_limit_bytes=56 * 1024 * 1024
        ),
        cost_estimate=pl.CostEstimate(
            flops=2 * TOK * D * HID, bytes_accessed=2 * (D * HID + 3 * TOK * HID), transcendentals=0
        ),
    )(
        frozen_base_matrix.T, *state_a, master_b, moment1_b, moment2_b,
        learner_token_inputs.T, learner_output_cotangents.T, rollout_inputs,
    )
    out, a_next, b_next = results[0], results[1:4], results[4:7]
    return (out.T, *[ref.T.reshape(RANK, 1, SHARE_A) for ref in a_next], *b_next)


def solution(mesh):
    state = P(None, "tensor", "group")
    return jax.shard_map(
        shards,
        mesh=mesh,
        in_specs=(P(None, "tensor"), *[state] * 6, P("group", "tensor"), P("group", "tensor"), P(("group", "tensor"), None)),
        out_specs=(P("group", "tensor"), *[state] * 6),
        check_vma=False,
    )
```

```python
import jax
import jax.numpy as jnp
from jax import lax
from jax.experimental import pallas as pl
from jax.experimental.pallas import tpu as pltpu
from jax.sharding import PartitionSpec as P

beta_one = 0.9
beta_two = 0.999
learn_rate = 0.001
adam_eps = 1e-08
adapter_scale = 2.0
fix_one = 0.9999734386011124
fix_two = 0.0952078528862904

MESH = pl.DeviceIdType.MESH
BF = jnp.bfloat16
F32 = jnp.float32

D, HID, TOK, COLS, ROWS = 5120, 1600, 512, 320, 32
SHARE_A, SHARE_B, RANK = 40, 200, 64
NT, NG = 16, 8

TENSOR_STEPS = sorted(
    ((dx, dy, dc) for dx in range(2) for dy in range(4) for dc in range(2) if (dx, dy, dc) != (0, 0, 0)),
    key=lambda s: -(s[0] + min(s[1], 4 - s[1]) + 0.1 * s[2]),
)
GROUP_STEPS = sorted(
    ((dz, dx) for dz in range(4) for dx in range(2) if (dz, dx) != (0, 0)),
    key=lambda s: -(min(s[0], 4 - s[0]) + 2 * s[1]),
)


def dot(left, right, left_dim, right_dim):
    return lax.dot_general(
        left, right, (((left_dim,), (right_dim,)), ((), ())), preferred_element_type=F32
    )


def aligned(index, size):
    return pl.ds(pl.multiple_of(index * size, size), size)


def kernel(
    base_hbm, ma_hbm, m1a_hbm, m2a_hbm, mb_hbm, m1b_hbm, m2b_hbm, xt_hbm, cot_hbm, xr_hbm,
    acc, b_left, b_right, xa, a_state, b_state,
    base, xt, cot, xall, a_in, b_in, pad, msg0, got0, msg0b, mom_a, mom_b,
    old_a, old_b, part, got1, low, own2, grad_b, grad_a, msg3a, got3a, msg3b, got3b, msg4, got4, b_rows, rows_b,
    a_left, a_right, cross, window_x, part5, got5, own5,
    loc, s0, r0, s0b, r0b, s1, r1, s2, r2, s3a, r3a, s3b, r3b, s4, r4, s5, r5, s6, r6, sx, rx, sc, rc, sw, rw,
):
    g = lax.axis_index("group")
    t = lax.axis_index("tensor")
    z, far = g // 2, lax.rem(g, 2)
    xl, y, core = t // 8, lax.rem(t // 2, 4), lax.rem(t, 2)

    def tensor_at(dx, dy, dc):
        return lax.rem(xl + dx, 2) * 8 + lax.rem(y + dy, 4) * 2 + lax.rem(core + dc, 2)

    def group_at(dz, dx):
        return lax.rem(z + dz, 4) * 2 + lax.rem(far + dx, 2)

    tensor_peers = [tensor_at(*s) for s in TENSOR_STEPS]
    group_peers = [group_at(*s) for s in GROUP_STEPS]

    bar = pltpu.get_barrier_semaphore()
    for gg in group_peers:
        pl.semaphore_signal(bar, inc=1, device_id=(gg, t), device_id_type=MESH)
    for tt in tensor_peers:
        pl.semaphore_signal(bar, inc=1, device_id=(g, tt), device_id_type=MESH)

    def remote(src, dst, ssem, rsem, k, gg, tt):
        copy = pltpu.make_async_remote_copy(
            src_ref=src, dst_ref=dst, send_sem=ssem.at[k], recv_sem=rsem.at[k],
            device_id=(gg, tt), device_id_type=MESH,
        )
        copy.start()
        return copy

    def load(src, dst, k):
        copy = pltpu.make_async_copy(src, dst, loc.at[k])
        copy.start()
        return copy

    load_b = load(mb_hbm, b_in.at[0], 0)
    load_a = load(ma_hbm, a_in.at[0], 1)
    mine = aligned(t, ROWS)
    load_x = load(xr_hbm, xall.at[mine], 2)
    load_cot = load(cot_hbm, cot, 3)
    load_xt = load(xt_hbm, xt, 4)
    loads_m = [
        load(m1b_hbm, b_in.at[1], 5), load(m2b_hbm, b_in.at[2], 6),
        load(m1a_hbm, a_in.at[1], 7), load(m2a_hbm, a_in.at[2], 8),
    ]
    load_base = load(base_hbm, base, 9)

    pad[...] = jnp.zeros_like(pad)
    msg0[...] = jnp.zeros_like(msg0)
    load_a.wait()
    pad[0, 0:SHARE_A, 0:RANK] = a_in[0]
    factor_a = pad[0].T[0:RANK, 0:SHARE_A]
    msg0[:, SHARE_B:SHARE_B + SHARE_A] = factor_a.astype(BF)
    load_b.wait()
    msg0[:, 0:SHARE_B] = b_in[0, :, 0, :].astype(BF)
    pl.semaphore_wait(bar, len(group_peers) + len(tensor_peers))
    copies0 = [remote(msg0, got0.at[g], s0, r0, k, gg, t) for k, gg in enumerate(group_peers)]
    got0[g] = msg0[...]

    x_next, y_up, y_down, sibling = tensor_at(1, 0, 0), tensor_at(0, 1, 0), tensor_at(0, 3, 0), tensor_at(0, 0, 1)
    half = D // 2
    low_half, high_half, all_of = pl.ds(0, half), pl.ds(half, half), pl.ds(0, D)

    def send_x(owner, columns, k, to):
        where = xall.at[aligned(owner, ROWS), columns]
        return remote(where, where, sx, rx, k, g, to)

    def share_x(owner, k):
        where = xall.at[aligned(owner, ROWS)]
        return remote(where, where, sc, rc, k, g, sibling)

    def window_of(tt):
        return pl.ds(pl.multiple_of((tt // 2) * 640 + lax.rem(tt, 2) * 256, 128), 384)

    load_x.wait()
    step1 = [send_x(t, all_of, 0, x_next), send_x(t, all_of, 1, y_up), send_x(t, all_of, 2, y_down)]
    shared = [share_x(t, 0)]
    far_chip = [tensor_at(1, 2, 0), tensor_at(1, 2, 1)]
    early = [
        remote(xall.at[mine, window_of(tt)], cross.at[k], sw, rw, k, g, tt) for k, tt in enumerate(far_chip)
    ]

    lanes = lax.broadcasted_iota(jnp.int32, (160, 128), 1)
    left = lanes < RANK

    def beside(first, second):
        rows = first.shape[0]
        return jnp.where(left[0:rows], first, pltpu.roll(second, RANK, 1))

    for copy in loads_m:
        copy.wait()
    for i in range(3):
        pad[1, 0:RANK, 0:128] = b_in[i, :, 0, 0:128]
        pad[2, 0:RANK, 0:SHARE_B - 128] = b_in[i, :, 0, 128:SHARE_B]
        rows_b[0:128, :] = pad[1].T
        rows_b[128:256, :] = pad[2].T
        mom_b[i] = beside(rows_b[0:112, :], rows_b[104:216, :])
    a_left[...] = jnp.zeros_like(a_left)
    a_right[...] = jnp.zeros_like(a_right)
    grad_b[HID:HID + 16, :] = jnp.zeros((16, 128), F32)
    msg0b[...] = jnp.zeros_like(msg0b)
    msg0b[0, :, 0:RANK] = a_in[1]
    msg0b[0, :, RANK:2 * RANK] = a_in[0]
    msg0b[1, :, RANK:2 * RANK] = a_in[2]
    rows_a = aligned(g, SHARE_A)
    mom_a[:, rows_a, :] = msg0b[...]

    for copy in copies0:
        copy.wait_recv()
    for j in range(NG):
        old_b[:, j * SHARE_B:(j + 1) * SHARE_B] = got0[j, :, 0:SHARE_B]
        old_a[:, j * SHARE_A:(j + 1) * SHARE_A] = got0[j, :, SHARE_B:SHARE_B + SHARE_A]
    load_cot.wait()
    load_xt.wait()
    hidden = dot(old_a[...], xt[...], 1, 0)
    back = dot(old_b[...], cot[...], 1, 0)
    for h in range(2):
        part[h, 0:RANK, :] = hidden[:, h * 256:(h + 1) * 256].astype(BF)
        part[h, RANK:, :] = back[:, h * 256:(h + 1) * 256].astype(BF)
    copies1 = [
        remote(part.at[lax.rem(tt, 2), aligned(tt // 2, 16)], got1.at[k], s1, r1, k, g, tt)
        for k, tt in enumerate(tensor_peers)
    ]

    copies0b = [
        remote(msg0b, mom_a.at[:, rows_a, :], s0b, r0b, k, gg, t) for k, gg in enumerate(group_peers)
    ]

    for copy in copies1:
        copy.wait_recv()
    my_half, my_rows = lax.rem(t, 2), aligned(t // 2, 16)
    total = part[my_half, my_rows, :].astype(F32)
    for k in range(NT - 1):
        total = total + got1[k].astype(F32)
    own2[...] = total.astype(BF)
    copies2 = [
        remote(own2, low.at[my_half, my_rows], s2, r2, k, g, tt) for k, tt in enumerate(tensor_peers)
    ]
    low[my_half, my_rows, :] = own2[...]

    for copy in step1:
        copy.wait_recv()
    of_x, of_up, of_down = x_next, y_up, y_down
    step2 = [
        send_x(of_x, high_half, 5, y_up),
        send_x(of_x, high_half, 6, y_down),
        send_x(of_up, low_half, 3, x_next),
        send_x(of_down, low_half, 4, x_next),
        send_x(of_down, low_half, 7, y_up),
        send_x(of_up, high_half, 8, y_down),
    ]
    shared += [share_x(of_x, 1), share_x(of_up, 2), share_x(of_down, 3)]

    for copy in copies2:
        copy.wait_recv()

    low0, low1 = low[0], low[1]
    grad_a[...] = dot(xt[:, 0:256], low0, 1, 1) + dot(xt[:, 256:512], low1, 1, 1)
    msg3a[...] = jnp.where(left, pltpu.roll(grad_a[0:160, :], RANK, 1), grad_a[160:320, :]).astype(BF)
    copies3a = [remote(msg3a, got3a.at[g], s3a, r3a, k, gg, t) for k, gg in enumerate(group_peers)]
    got3a[g] = msg3a[...]

    def grad_rows(i, carry):
        rows = aligned(i, 400)
        grad_b[rows, :] = dot(cot[rows, 0:256], low0, 1, 1) + dot(cot[rows, 256:512], low1, 1, 1)
        return carry

    lax.fori_loop(0, HID // 400, grad_rows, 0)

    def message3(j):
        return beside(
            grad_b[pl.ds(pl.multiple_of(j * SHARE_B, 8), 112), :],
            grad_b[pl.ds(pl.multiple_of(j * SHARE_B + 104, 8), 112), :],
        ).astype(BF)

    copies3b = []
    for k, gg in enumerate(group_peers):
        msg3b[k] = message3(gg)
        copies3b.append(remote(msg3b.at[k], got3b.at[g], s3b, r3b, k, gg, t))
    got3b[g] = message3(g)

    for copy in copies0b:
        copy.wait_recv()

    def packed_right(rows):
        return jnp.where(left, pltpu.roll(rows[0:160], RANK, 1), rows[160:320])

    master_a = packed_right(mom_a[0])
    second_a = packed_right(mom_a[1])
    first_a = beside(mom_a[0, 0:160, :], mom_a[0, 160:320, :])

    for copy in step2:
        copy.wait_recv()
    across = tensor_at(0, 2, 0)
    quarter = D // 4
    step3 = [
        send_x(across, low_half, 9, x_next),
        send_x(tensor_at(1, 1, 0), pl.ds(2 * quarter, quarter), 10, y_down),
        send_x(tensor_at(1, 3, 0), pl.ds(3 * quarter, quarter), 11, y_up),
    ]
    shared += [share_x(across, 4), share_x(tensor_at(1, 1, 0), 5), share_x(tensor_at(1, 3, 0), 6)]

    def base_rows(h, first, last):
        tokens = aligned(h, 256)

        def body(i, carry):
            rows = aligned(i, 800)
            acc[h, rows, :] = dot(base[rows, :], xall[tokens, :], 1, 1)
            return carry

        lax.fori_loop(first, last, body, 0)

    def adam(master, first, second, got):
        grad = got[0].astype(F32)
        for j in range(1, NG):
            grad = grad + got[j].astype(F32)
        grad = adapter_scale * grad
        first_next = beta_one * first + (1.0 - beta_one) * grad
        second_next = beta_two * second + (1.0 - beta_two) * grad * grad
        master_next = master - learn_rate * (first_next / fix_one) / (
            jnp.sqrt(second_next / fix_two) + adam_eps
        )
        return master_next, first_next, second_next

    load_base.wait()
    for k in (0, 2, 3, 4):
        shared[k].wait_recv()
    base_rows(xl, 0, 1)

    for copy in copies3a:
        copy.wait_recv()
    next_a = adam(master_a, first_a, second_a, got3a)
    new_a = next_a[0].astype(BF).astype(F32)
    turned = pltpu.roll(new_a, RANK, 1)
    place = pl.multiple_of(core * RANK, RANK)
    a_left[pl.ds(place, 160), :] = jnp.where(left, new_a, 0.0).astype(BF)
    a_left[pl.ds(place + 160, 160), :] = jnp.where(left, turned, 0.0).astype(BF)
    a_right[pl.ds(place, 160), :] = jnp.where(left, 0.0, turned).astype(BF)
    a_right[pl.ds(place + 160, 160), :] = jnp.where(left, 0.0, new_a).astype(BF)

    for k in (1, 5, 6):
        shared[k].wait_recv()
    for copy in early:
        copy.wait_recv()
    own_window = window_of(t)
    for dx in range(2):
        for dy in range(4):
            for dc in range(2):
                rows = aligned(tensor_at(dx, dy, dc), ROWS)
                window_x[rows, :] = cross[dc] if (dx, dy) == (1, 2) else xall[rows, own_window]
    part5[...] = (
        dot(window_x[0:256, :], a_left[...], 1, 0) + dot(window_x[256:512, :], a_right[...], 1, 0)
    ).astype(BF)
    copies5 = [
        remote(part5.at[aligned(tt, 16)], got5.at[k], s5, r5, k, g, tt)
        for k, tt in enumerate(tensor_peers)
    ]

    for copy in copies3b:
        copy.wait_recv()
    next_b = adam(mom_b[0], mom_b[1], mom_b[2], got3b)
    msg4[...] = next_b[0].astype(BF)
    copies4 = [remote(msg4, got4.at[g], s4, r4, k, gg, t) for k, gg in enumerate(group_peers)]
    got4[g] = msg4[...]

    for copy in step3:
        copy.wait_recv()
    shared.append(share_x(tensor_at(1, 2, 0), 7))

    base_rows(xl, 1, 2)

    for copy in copies5:
        copy.wait_recv()
    mine5 = aligned(t, 16)
    total = part5[mine5, :].astype(F32)
    for k in range(NT - 1):
        total = total + got5[k].astype(F32)
    own5[...] = (adapter_scale * total).astype(BF)
    copies6 = [remote(own5, xa.at[mine5], s6, r6, k, g, tt) for k, tt in enumerate(tensor_peers)]
    xa[mine5, :] = own5[...]

    shared[7].wait_recv()
    base_rows(1 - xl, 0, 2)

    rows_out = aligned(lax.rem(g, 4), SHARE_A)
    for i in range(3):
        grad_a[0:160, :] = next_a[i]
        own_rows = grad_a[rows_out, :]
        own_rows = jnp.where(g < 4, own_rows, pltpu.roll(own_rows, RANK, 1))
        a_state[i] = own_rows[:, 0:RANK]
        rows_b[0:104, :] = next_b[i][0:104]
        rows_b[104:200, :] = pltpu.roll(next_b[i], RANK, 1)[0:96]
        b_state[i, :, 0, 0:128] = rows_b[0:128, :].T[0:RANK]
        b_state[i, :, 0, 128:SHARE_B] = rows_b[128:256, :].T[0:RANK, 0:SHARE_B - 128]

    for copy in copies4:
        copy.wait_recv()
    for j in range(NG):
        rows = got4[j].astype(F32)
        b_rows[j * SHARE_B:j * SHARE_B + 104, :] = jnp.where(left[0:104], rows[0:104], 0.0)
        b_rows[j * SHARE_B + 104:(j + 1) * SHARE_B, :] = jnp.where(
            left[0:96], pltpu.roll(rows, RANK, 1)[0:96], 0.0
        )
    b_left[...] = b_rows[...].astype(BF)
    b_right[...] = pltpu.roll(b_rows[...], RANK, 1).astype(BF)

    for copy in copies6:
        copy.wait_recv()
    for group in (
        copies0, step1, shared, early, copies0b, copies1, step2, copies2, copies3a, copies3b, step3, copies4, copies5, copies6,
    ):
        for copy in group:
            copy.wait_send()


def finish(
    acc, b_left, b_right, xa, a_state, b_state,
    out_hbm, ma_out, m1a_out, m2a_out, mb_out, m1b_out, m2b_out,
    out_v, sem,
):
    def store(src, dst, k):
        copy = pltpu.make_async_copy(src, dst, sem.at[k])
        copy.start()
        return copy

    stores = []
    for i in range(5):
        rows = pl.ds(320 * i, 320)
        out_v[rows, 0:256] = (acc[0, rows, :] + dot(b_left[rows, :], xa[...], 1, 1)).astype(BF)
        out_v[rows, 256:512] = (acc[1, rows, :] + dot(b_right[rows, :], xa[...], 1, 1)).astype(BF)
        stores.append(store(out_v.at[rows], out_hbm.at[rows], i))
        if i == 0:
            stores += [store(a_state.at[j], ref, 5 + j) for j, ref in enumerate((ma_out, m1a_out, m2a_out))]
            stores += [store(b_state.at[j], ref, 8 + j) for j, ref in enumerate((mb_out, m1b_out, m2b_out))]
    for copy in stores:
        copy.wait()


def shards(
    frozen_base_matrix, master_a, moment1_a, moment2_a, master_b, moment1_b, moment2_b,
    learner_token_inputs, learner_output_cotangents, rollout_inputs,
):
    state_a = [ref.reshape(RANK, SHARE_A).T for ref in (master_a, moment1_a, moment2_a)]
    dma = pltpu.SemaphoreType.DMA
    vmem = pltpu.VMEM
    any_space = pl.BlockSpec(memory_space=pl.ANY)
    in_vmem = pl.BlockSpec(memory_space=pltpu.VMEM)
    shape = jax.ShapeDtypeStruct
    mib = 1024 * 1024
    operands = (
        frozen_base_matrix.T, *state_a, master_b, moment1_b, moment2_b,
        learner_token_inputs.T, learner_output_cotangents.T, rollout_inputs,
    )
    parts = pl.pallas_call(
        kernel,
        out_shape=[
            vmem((2, HID, 256), F32),
            vmem((HID, 128), BF),
            vmem((HID, 128), BF),
            vmem((256, 128), BF),
            vmem((3, SHARE_A, RANK), F32),
            vmem((3, RANK, 1, SHARE_B), F32),
        ],
        in_specs=[any_space] * 10,
        out_specs=[in_vmem] * 6,
        scratch_shapes=[
            vmem((HID, D), BF),
            vmem((COLS, TOK), BF),
            vmem((HID, TOK), BF),
            vmem((TOK, D), BF),
            vmem((3, SHARE_A, RANK), F32),
            vmem((3, RANK, 1, SHARE_B), F32),
            vmem((3, 128, 128), F32),
            vmem((RANK, 256), BF),
            vmem((NG, RANK, 256), BF),
            vmem((2, SHARE_A, 128), F32),
            vmem((2, COLS, 128), F32),
            vmem((3, 112, 128), F32),
            vmem((RANK, COLS), BF),
            vmem((RANK, HID), BF),
            vmem((2, 128, 256), BF),
            vmem((NT - 1, 16, 256), BF),
            vmem((2, 128, 256), BF),
            vmem((16, 256), BF),
            vmem((HID + 16, 128), F32),
            vmem((COLS, 128), F32),
            vmem((160, 128), BF),
            vmem((NG, 160, 128), BF),
            vmem((NG - 1, 112, 128), BF),
            vmem((NG, 112, 128), BF),
            vmem((112, 128), BF),
            vmem((NG, 112, 128), BF),
            vmem((HID, 128), F32),
            vmem((256, 128), F32),
            vmem((384, 128), BF),
            vmem((384, 128), BF),
            vmem((2, ROWS, 384), BF),
            vmem((TOK, 384), BF),
            vmem((256, 128), BF),
            vmem((NT - 1, 16, 128), BF),
            vmem((16, 128), BF),
            dma((10,)),
        ]
        + [dma((n,)) for n in (7, 7, 7, 7, 15, 15, 15, 15, 7, 7, 7, 7, 7, 7, 15, 15, 15, 15, 12, 12, 8, 8, 2, 2)],
        compiler_params=pltpu.CompilerParams(
            collective_id=0, has_side_effects=True, vmem_limit_bytes=44 * mib
        ),
        cost_estimate=pl.CostEstimate(
            flops=2 * TOK * D * HID, bytes_accessed=2 * (D * HID + 2 * TOK * HID), transcendentals=0
        ),
    )(*[pltpu.with_memory_space_constraint(operand, pltpu.HBM) for operand in operands])
    results = pl.pallas_call(
        finish,
        out_shape=[shape((HID, TOK), BF)]
        + [shape((SHARE_A, RANK), F32)] * 3
        + [shape((RANK, 1, SHARE_B), F32)] * 3,
        in_specs=[in_vmem] * 6,
        out_specs=[any_space] * 7,
        scratch_shapes=[vmem((HID, TOK), BF), dma((11,))],
        compiler_params=pltpu.CompilerParams(vmem_limit_bytes=10 * mib),
        cost_estimate=pl.CostEstimate(
            flops=2 * TOK * RANK * HID, bytes_accessed=2 * TOK * HID, transcendentals=0
        ),
    )(*parts)
    out, a_next, b_next = results[0], results[1:4], results[4:7]
    return (out.T, *[ref.T.reshape(RANK, 1, SHARE_A) for ref in a_next], *b_next)


def solution(mesh):
    state = P(None, "tensor", "group")
    return jax.shard_map(
        shards,
        mesh=mesh,
        in_specs=(P(None, "tensor"), *[state] * 6, P("group", "tensor"), P("group", "tensor"), P(("group", "tensor"), None)),
        out_specs=(P("group", "tensor"), *[state] * 6),
        check_vma=False,
    )
```

```python
import jax
import jax.numpy as jnp
from jax import lax
from jax.experimental import pallas as pl
from jax.experimental.pallas import tpu as pltpu
from jax.sharding import PartitionSpec as P

beta_one = 0.9
beta_two = 0.999
learn_rate = 0.001
adam_eps = 1e-08
adapter_scale = 2.0
fix_one = 0.9999734386011124
fix_two = 0.0952078528862904

MESH = pl.DeviceIdType.MESH
BF = jnp.bfloat16
F32 = jnp.float32

D, HID, TOK, COLS, ROWS = 5120, 1600, 512, 320, 32
SHARE_A, SHARE_B, RANK = 40, 200, 64
NT, NG = 16, 8

TENSOR_STEPS = sorted(
    ((dx, dy, dc) for dx in range(2) for dy in range(4) for dc in range(2) if (dx, dy, dc) != (0, 0, 0)),
    key=lambda s: -(s[0] + min(s[1], 4 - s[1]) + 0.1 * s[2]),
)
GROUP_STEPS = sorted(
    ((dz, dx) for dz in range(4) for dx in range(2) if (dz, dx) != (0, 0)),
    key=lambda s: -(min(s[0], 4 - s[0]) + 2 * s[1]),
)


def dot(left, right, left_dim, right_dim):
    return lax.dot_general(
        left, right, (((left_dim,), (right_dim,)), ((), ())), preferred_element_type=F32
    )


def aligned(index, size):
    return pl.ds(pl.multiple_of(index * size, size), size)


def kernel(
    base_hbm, ma_hbm, m1a_hbm, m2a_hbm, mb_hbm, m1b_hbm, m2b_hbm, xt_hbm, cot_hbm, xr_hbm,
    acc, b_left, b_right, xa, a_state, b_state,
    base, xt, cot, xall, a_in, b_in, pad, msg0, got0, msg0b, mom_a, mom_b,
    old_a, old_b, part, got1, low, own2, grad_b, grad_a, msg3a, got3a, msg3b, got3b, msg4, got4, b_rows, rows_b,
    a_left, a_right, cross, window_x, part5, got5, own5,
    loc, s0, r0, s0b, r0b, s1, r1, s2, r2, s3a, r3a, s3b, r3b, s4, r4, s5, r5, s6, r6, sx, rx, sc, rc, sw, rw,
):
    g = lax.axis_index("group")
    t = lax.axis_index("tensor")
    z, far = g // 2, lax.rem(g, 2)
    xl, y, core = t // 8, lax.rem(t // 2, 4), lax.rem(t, 2)

    def tensor_at(dx, dy, dc):
        return lax.rem(xl + dx, 2) * 8 + lax.rem(y + dy, 4) * 2 + lax.rem(core + dc, 2)

    def group_at(dz, dx):
        return lax.rem(z + dz, 4) * 2 + lax.rem(far + dx, 2)

    tensor_peers = [tensor_at(*s) for s in TENSOR_STEPS]
    group_peers = [group_at(*s) for s in GROUP_STEPS]

    bar = pltpu.get_barrier_semaphore()
    for gg in group_peers:
        pl.semaphore_signal(bar, inc=1, device_id=(gg, t), device_id_type=MESH)
    for tt in tensor_peers:
        pl.semaphore_signal(bar, inc=1, device_id=(g, tt), device_id_type=MESH)

    def remote(src, dst, ssem, rsem, k, gg, tt):
        copy = pltpu.make_async_remote_copy(
            src_ref=src, dst_ref=dst, send_sem=ssem.at[k], recv_sem=rsem.at[k],
            device_id=(gg, tt), device_id_type=MESH,
        )
        copy.start()
        return copy

    def load(src, dst, k):
        copy = pltpu.make_async_copy(src, dst, loc.at[k])
        copy.start()
        return copy

    load_b = load(mb_hbm, b_in.at[0], 0)
    load_a = load(ma_hbm, a_in.at[0], 1)

    def slot(at_y, dx, dy):
        place = lax.rem(at_y + (2 if (dx, dy) == (1, 0) or (dx, dy) == (0, 2) else 0) + dy, 4)
        late = (dx, dy) == (0, 2) or (dx == 1 and dy != 0)
        return (8 if late else 0) + place * 2

    def rows_of(dx, dy, at_core=core, at_y=y):
        return aligned(slot(at_y, dx, dy) + at_core, ROWS)

    mine = rows_of(0, 0)
    load_x = load(xr_hbm, xall.at[mine], 2)
    load_cot = load(cot_hbm, cot, 3)
    load_xt = load(xt_hbm, xt, 4)
    loads_m = [
        load(m1b_hbm, b_in.at[1], 5), load(m2b_hbm, b_in.at[2], 6),
        load(m1a_hbm, a_in.at[1], 7), load(m2a_hbm, a_in.at[2], 8),
    ]
    load_base = load(base_hbm, base, 9)

    pad[...] = jnp.zeros_like(pad)
    msg0[...] = jnp.zeros_like(msg0)
    load_a.wait()
    pad[0, 0:SHARE_A, 0:RANK] = a_in[0]
    factor_a = pad[0].T[0:RANK, 0:SHARE_A]
    msg0[:, SHARE_B:SHARE_B + SHARE_A] = factor_a.astype(BF)
    load_b.wait()
    msg0[:, 0:SHARE_B] = b_in[0, :, 0, :].astype(BF)
    pl.semaphore_wait(bar, len(group_peers) + len(tensor_peers))
    copies0 = [remote(msg0, got0.at[g], s0, r0, k, gg, t) for k, gg in enumerate(group_peers)]
    got0[g] = msg0[...]

    x_next, y_up, y_down, sibling = tensor_at(1, 0, 0), tensor_at(0, 1, 0), tensor_at(0, 3, 0), tensor_at(0, 0, 1)
    half, quarter = D // 2, D // 4
    own_half, other_half = xl, 1 - xl
    sent_x, sent_share = [], []

    def columns_of(first, count=1):
        return pl.ds(pl.multiple_of(first * quarter, quarter), count * quarter)

    def half_of(i):
        return pl.ds(pl.multiple_of(i * half, half), half)

    def send_x(here, there, at_y, columns, to):
        copy = remote(
            xall.at[rows_of(*here), columns], xall.at[rows_of(*there, at_y=at_y), columns],
            sx, rx, len(sent_x), g, to,
        )
        sent_x.append(copy)
        return copy

    def share_x(here, columns):
        where = xall.at[rows_of(*here), columns]
        copy = remote(where, where, sc, rc, len(sent_share), g, sibling)
        sent_share.append(copy)
        return copy

    def arrived(copies):
        for copy in copies:
            copy.wait_recv()

    everything = pl.ds(0, D)

    def window_of(tt):
        return pl.ds(pl.multiple_of((tt // 2) * 640 + lax.rem(tt, 2) * 256, 128), 384)

    load_x.wait()
    step_a = [
        send_x((0, 0), (0, 3), y + 1, columns_of(0, 3), y_up),
        send_x((0, 0), (0, 1), y + 3, columns_of(1, 3), y_down),
        send_x((0, 0), (1, 0), y, half_of(other_half), x_next),
    ]
    near = [share_x((0, 0), everything)]

    lanes = lax.broadcasted_iota(jnp.int32, (160, 128), 1)
    left = lanes < RANK

    def beside(first, second):
        rows = first.shape[0]
        return jnp.where(left[0:rows], first, pltpu.roll(second, RANK, 1))

    for copy in loads_m:
        copy.wait()
    for i in range(3):
        pad[1, 0:RANK, 0:128] = b_in[i, :, 0, 0:128]
        pad[2, 0:RANK, 0:SHARE_B - 128] = b_in[i, :, 0, 128:SHARE_B]
        rows_b[0:128, :] = pad[1].T
        rows_b[128:256, :] = pad[2].T
        mom_b[i] = beside(rows_b[0:112, :], rows_b[104:216, :])
    a_left[...] = jnp.zeros_like(a_left)
    a_right[...] = jnp.zeros_like(a_right)
    grad_b[HID:HID + 16, :] = jnp.zeros((16, 128), F32)
    msg0b[...] = jnp.zeros_like(msg0b)
    msg0b[0, :, 0:RANK] = a_in[1]
    msg0b[0, :, RANK:2 * RANK] = a_in[0]
    msg0b[1, :, RANK:2 * RANK] = a_in[2]
    rows_a = aligned(g, SHARE_A)
    mom_a[:, rows_a, :] = msg0b[...]

    for copy in copies0:
        copy.wait_recv()
    for j in range(NG):
        old_b[:, j * SHARE_B:(j + 1) * SHARE_B] = got0[j, :, 0:SHARE_B]
        old_a[:, j * SHARE_A:(j + 1) * SHARE_A] = got0[j, :, SHARE_B:SHARE_B + SHARE_A]
    load_cot.wait()
    load_xt.wait()
    hidden = dot(old_a[...], xt[...], 1, 0)
    back = dot(old_b[...], cot[...], 1, 0)
    for h in range(2):
        part[h, 0:RANK, :] = hidden[:, h * 256:(h + 1) * 256].astype(BF)
        part[h, RANK:, :] = back[:, h * 256:(h + 1) * 256].astype(BF)
    copies1 = [
        remote(part.at[lax.rem(tt, 2), aligned(tt // 2, 16)], got1.at[k], s1, r1, k, g, tt)
        for k, tt in enumerate(tensor_peers)
    ]

    step_b = [
        send_x((0, 0), (0, 3), y + 1, columns_of(3), y_up),
        send_x((0, 0), (0, 1), y + 3, columns_of(0), y_down),
        send_x((0, 0), (1, 0), y, half_of(own_half), x_next),
    ]

    partner = group_at(0, 1)
    z_peers = [group_at(dz, 0) for dz in (2, 1, 3)]
    copies0b = [
        remote(msg0b, mom_a.at[:, rows_a, :], s0b, r0b, k, gg, t) for k, gg in enumerate([partner] + z_peers)
    ]

    for copy in copies1:
        copy.wait_recv()
    my_half, my_rows = lax.rem(t, 2), aligned(t // 2, 16)
    total = part[my_half, my_rows, :].astype(F32)
    for k in range(NT - 1):
        total = total + got1[k].astype(F32)
    own2[...] = total.astype(BF)
    copies2 = [
        remote(own2, low.at[my_half, my_rows], s2, r2, k, g, tt) for k, tt in enumerate(tensor_peers)
    ]
    low[my_half, my_rows, :] = own2[...]

    arrived(step_a)
    early = []
    for dy in (2, 1, 3):
        for dc in range(2):
            to = tensor_at(0, dy, dc)
            k = 2 * (dy - 1) + dc
            early.append(
                remote(xall.at[rows_of(1, 0), window_of(to)], cross.at[k], sw, rw, k, g, to)
            )
    step_c = [
        send_x((0, 3), (0, 2), y + 1, columns_of(0, 2), y_up),
        send_x((0, 1), (0, 2), y + 3, columns_of(2, 2), y_down),
    ]
    step_d = [
        send_x((1, 0), (1, 3), y + 1, half_of(own_half), y_up),
        send_x((1, 0), (1, 1), y + 3, half_of(own_half), y_down),
    ]
    step_e = [
        send_x((0, 1), (1, 1), y, columns_of(2 * own_half + 1), x_next),
        send_x((0, 3), (1, 3), y, columns_of(2 * own_half), x_next),
    ]
    arrived(step_b)
    near += [share_x(there, everything) for there in ((1, 0), (0, 1), (0, 3))]
    copies0b[0].wait_recv()
    rows_partner = aligned(partner, SHARE_A)
    copies0b += [
        remote(mom_a.at[:, rows_partner, :], mom_a.at[:, rows_partner, :], s0b, r0b, 4 + k, gg, t)
        for k, gg in enumerate(z_peers)
    ]

    for copy in copies2:
        copy.wait_recv()

    low0, low1 = low[0], low[1]
    grad_a[...] = dot(xt[:, 0:256], low0, 1, 1) + dot(xt[:, 256:512], low1, 1, 1)
    msg3a[...] = jnp.where(left, pltpu.roll(grad_a[0:160, :], RANK, 1), grad_a[160:320, :]).astype(BF)
    copies3a = [remote(msg3a, got3a.at[g], s3a, r3a, k, gg, t) for k, gg in enumerate(group_peers)]
    got3a[g] = msg3a[...]

    def grad_rows(i, carry):
        rows = aligned(i, 400)
        grad_b[rows, :] = dot(cot[rows, 0:256], low0, 1, 1) + dot(cot[rows, 256:512], low1, 1, 1)
        return carry

    lax.fori_loop(0, HID // 400, grad_rows, 0)

    def message3(j):
        return beside(
            grad_b[pl.ds(pl.multiple_of(j * SHARE_B, 8), 112), :],
            grad_b[pl.ds(pl.multiple_of(j * SHARE_B + 104, 8), 112), :],
        ).astype(BF)

    copies3b = []
    for k, gg in enumerate(group_peers):
        msg3b[k] = message3(gg)
        copies3b.append(remote(msg3b.at[k], got3b.at[g], s3b, r3b, k, gg, t))
    got3b[g] = message3(g)

    arrived(copies0b[1:])

    def packed_right(rows):
        return jnp.where(left, pltpu.roll(rows[0:160], RANK, 1), rows[160:320])

    master_a = packed_right(mom_a[0])
    second_a = packed_right(mom_a[1])
    first_a = beside(mom_a[0, 0:160, :], mom_a[0, 160:320, :])

    def base_rows(part, first, last):
        def body(i, carry):
            rows = aligned(i, 800)
            acc[part, rows, :] = dot(base[rows, :], xall[part * 256:(part + 1) * 256, :], 1, 1)
            return carry

        lax.fori_loop(first, last, body, 0)

    load_base.wait()
    arrived(near)
    base_rows(0, 0, 1)

    arrived(step_c)
    two_away = share_x((0, 2), everything)

    def adam(master, first, second, got):
        grad = got[0].astype(F32)
        for j in range(1, NG):
            grad = grad + got[j].astype(F32)
        grad = adapter_scale * grad
        first_next = beta_one * first + (1.0 - beta_one) * grad
        second_next = beta_two * second + (1.0 - beta_two) * grad * grad
        master_next = master - learn_rate * (first_next / fix_one) / (
            jnp.sqrt(second_next / fix_two) + adam_eps
        )
        return master_next, first_next, second_next

    for copy in copies3a:
        copy.wait_recv()
    next_a = adam(master_a, first_a, second_a, got3a)
    new_a = next_a[0].astype(BF).astype(F32)
    turned = pltpu.roll(new_a, RANK, 1)
    place = pl.multiple_of(core * RANK, RANK)
    a_left[pl.ds(place, 160), :] = jnp.where(left, new_a, 0.0).astype(BF)
    a_left[pl.ds(place + 160, 160), :] = jnp.where(left, turned, 0.0).astype(BF)
    a_right[pl.ds(place, 160), :] = jnp.where(left, 0.0, turned).astype(BF)
    a_right[pl.ds(place + 160, 160), :] = jnp.where(left, 0.0, new_a).astype(BF)

    arrived(early + [two_away])
    own_window = window_of(t)
    for dx in range(2):
        for dy in range(4):
            for dc in range(2):
                rows = aligned(tensor_at(dx, dy, dc), ROWS)
                held = rows_of(dx, dy, lax.rem(core + dc, 2))
                window_x[rows, :] = cross[2 * ((4 - dy) - 1) + dc] if dx == 1 and dy else xall[held, own_window]
    part5[...] = (
        dot(window_x[0:256, :], a_left[...], 1, 0) + dot(window_x[256:512, :], a_right[...], 1, 0)
    ).astype(BF)
    copies5 = [
        remote(part5.at[aligned(tt, 16)], got5.at[k], s5, r5, k, g, tt)
        for k, tt in enumerate(tensor_peers)
    ]

    step_f = [
        send_x((1, 0), (1, 3), y + 1, columns_of(2 * other_half + 1), y_up),
        send_x((1, 0), (1, 1), y + 3, columns_of(2 * other_half), y_down),
        send_x((0, 2), (1, 2), y, half_of(own_half), x_next),
    ]

    for copy in copies3b:
        copy.wait_recv()
    next_b = adam(mom_b[0], mom_b[1], mom_b[2], got3b)
    msg4[...] = next_b[0].astype(BF)
    copies4 = [remote(msg4, got4.at[g], s4, r4, k, gg, t) for k, gg in enumerate(group_peers)]
    got4[g] = msg4[...]

    arrived(step_d + step_e)
    step_g = [
        send_x((1, 1), (1, 2), y + 3, columns_of(2 * own_half), y_down),
        send_x((1, 3), (1, 2), y + 1, columns_of(2 * own_half + 1), y_up),
    ]
    away = [share_x(there, half_of(own_half)) for there in ((1, 1), (1, 3))]

    base_rows(0, 1, 2)

    for copy in copies5:
        copy.wait_recv()
    mine5 = aligned(t, 16)
    total = part5[mine5, :].astype(F32)
    for k in range(NT - 1):
        total = total + got5[k].astype(F32)
    own5[...] = (adapter_scale * total).astype(BF)
    copies6 = [remote(own5, xa.at[mine5], s6, r6, k, g, tt) for k, tt in enumerate(tensor_peers)]
    xa[mine5, :] = own5[...]

    arrived(step_f + step_g)
    away += [share_x((1, 2), everything)] + [share_x(there, half_of(other_half)) for there in ((1, 1), (1, 3))]
    arrived(away)
    base_rows(1, 0, 2)

    rows_out = aligned(lax.rem(g, 4), SHARE_A)
    for i in range(3):
        grad_a[0:160, :] = next_a[i]
        own_rows = grad_a[rows_out, :]
        own_rows = jnp.where(g < 4, own_rows, pltpu.roll(own_rows, RANK, 1))
        a_state[i] = own_rows[:, 0:RANK]
        rows_b[0:104, :] = next_b[i][0:104]
        rows_b[104:200, :] = pltpu.roll(next_b[i], RANK, 1)[0:96]
        b_state[i, :, 0, 0:128] = rows_b[0:128, :].T[0:RANK]
        b_state[i, :, 0, 128:SHARE_B] = rows_b[128:256, :].T[0:RANK, 0:SHARE_B - 128]

    for copy in copies4:
        copy.wait_recv()
    for j in range(NG):
        rows = got4[j].astype(F32)
        b_rows[j * SHARE_B:j * SHARE_B + 104, :] = jnp.where(left[0:104], rows[0:104], 0.0)
        b_rows[j * SHARE_B + 104:(j + 1) * SHARE_B, :] = jnp.where(
            left[0:96], pltpu.roll(rows, RANK, 1)[0:96], 0.0
        )
    b_left[...] = b_rows[...].astype(BF)
    b_right[...] = pltpu.roll(b_rows[...], RANK, 1).astype(BF)

    for copy in copies6:
        copy.wait_recv()
    for group in (
        copies0, sent_x, sent_share, early, copies0b, copies1, copies2, copies3a, copies3b, copies4, copies5, copies6,
    ):
        for copy in group:
            copy.wait_send()


def finish(
    acc, b_left, b_right, xa, a_state, b_state,
    out_hbm, ma_out, m1a_out, m2a_out, mb_out, m1b_out, m2b_out,
    out_v, sem,
):
    def store(src, dst, k):
        copy = pltpu.make_async_copy(src, dst, sem.at[k])
        copy.start()
        return copy

    t = lax.axis_index("tensor")
    xl, y = t // 8, lax.rem(t // 2, 4)
    place = lax.broadcasted_iota(jnp.int32, (320, 256), 1) // 64
    from_late, from_early = place == lax.rem(y + 2, 4), place == y
    stores = []
    for i in range(5):
        rows = pl.ds(320 * i, 320)
        near, away = acc[0, rows, :], acc[1, rows, :]
        own = jnp.where(from_late, jnp.concatenate([away[:, 128:], away[:, :128]], axis=1), near)
        other = jnp.where(from_early, jnp.concatenate([near[:, 128:], near[:, :128]], axis=1), away)
        out_v[rows, 0:256] = (jnp.where(xl == 0, own, other) + dot(b_left[rows, :], xa[...], 1, 1)).astype(BF)
        out_v[rows, 256:512] = (jnp.where(xl == 0, other, own) + dot(b_right[rows, :], xa[...], 1, 1)).astype(BF)
        stores.append(store(out_v.at[rows], out_hbm.at[rows], i))
        if i == 0:
            stores += [store(a_state.at[j], ref, 5 + j) for j, ref in enumerate((ma_out, m1a_out, m2a_out))]
            stores += [store(b_state.at[j], ref, 8 + j) for j, ref in enumerate((mb_out, m1b_out, m2b_out))]
    for copy in stores:
        copy.wait()


def shards(
    frozen_base_matrix, master_a, moment1_a, moment2_a, master_b, moment1_b, moment2_b,
    learner_token_inputs, learner_output_cotangents, rollout_inputs,
):
    state_a = [ref.reshape(RANK, SHARE_A).T for ref in (master_a, moment1_a, moment2_a)]
    dma = pltpu.SemaphoreType.DMA
    vmem = pltpu.VMEM
    any_space = pl.BlockSpec(memory_space=pl.ANY)
    in_vmem = pl.BlockSpec(memory_space=pltpu.VMEM)
    shape = jax.ShapeDtypeStruct
    mib = 1024 * 1024
    operands = (
        frozen_base_matrix.T, *state_a, master_b, moment1_b, moment2_b,
        learner_token_inputs.T, learner_output_cotangents.T, rollout_inputs,
    )
    parts = pl.pallas_call(
        kernel,
        out_shape=[
            vmem((2, HID, 256), F32),
            vmem((HID, 128), BF),
            vmem((HID, 128), BF),
            vmem((256, 128), BF),
            vmem((3, SHARE_A, RANK), F32),
            vmem((3, RANK, 1, SHARE_B), F32),
        ],
        in_specs=[any_space] * 10,
        out_specs=[in_vmem] * 6,
        scratch_shapes=[
            vmem((HID, D), BF),
            vmem((COLS, TOK), BF),
            vmem((HID, TOK), BF),
            vmem((TOK, D), BF),
            vmem((3, SHARE_A, RANK), F32),
            vmem((3, RANK, 1, SHARE_B), F32),
            vmem((3, 128, 128), F32),
            vmem((RANK, 256), BF),
            vmem((NG, RANK, 256), BF),
            vmem((2, SHARE_A, 128), F32),
            vmem((2, COLS, 128), F32),
            vmem((3, 112, 128), F32),
            vmem((RANK, COLS), BF),
            vmem((RANK, HID), BF),
            vmem((2, 128, 256), BF),
            vmem((NT - 1, 16, 256), BF),
            vmem((2, 128, 256), BF),
            vmem((16, 256), BF),
            vmem((HID + 16, 128), F32),
            vmem((COLS, 128), F32),
            vmem((160, 128), BF),
            vmem((NG, 160, 128), BF),
            vmem((NG - 1, 112, 128), BF),
            vmem((NG, 112, 128), BF),
            vmem((112, 128), BF),
            vmem((NG, 112, 128), BF),
            vmem((HID, 128), F32),
            vmem((256, 128), F32),
            vmem((384, 128), BF),
            vmem((384, 128), BF),
            vmem((6, ROWS, 384), BF),
            vmem((TOK, 384), BF),
            vmem((256, 128), BF),
            vmem((NT - 1, 16, 128), BF),
            vmem((16, 128), BF),
            dma((10,)),
        ]
        + [dma((n,)) for n in (7, 7, 7, 7, 15, 15, 15, 15, 7, 7, 7, 7, 7, 7, 15, 15, 15, 15, 17, 17, 10, 10, 6, 6)],
        compiler_params=pltpu.CompilerParams(
            collective_id=0, has_side_effects=True, vmem_limit_bytes=44 * mib
        ),
        cost_estimate=pl.CostEstimate(
            flops=2 * TOK * D * HID, bytes_accessed=2 * (D * HID + 2 * TOK * HID), transcendentals=0
        ),
    )(*[pltpu.with_memory_space_constraint(operand, pltpu.HBM) for operand in operands])
    results = pl.pallas_call(
        finish,
        out_shape=[shape((HID, TOK), BF)]
        + [shape((SHARE_A, RANK), F32)] * 3
        + [shape((RANK, 1, SHARE_B), F32)] * 3,
        in_specs=[in_vmem] * 6,
        out_specs=[any_space] * 7,
        scratch_shapes=[vmem((HID, TOK), BF), dma((11,))],
        compiler_params=pltpu.CompilerParams(vmem_limit_bytes=10 * mib),
        cost_estimate=pl.CostEstimate(
            flops=2 * TOK * RANK * HID, bytes_accessed=2 * TOK * HID, transcendentals=0
        ),
    )(*parts)
    out, a_next, b_next = results[0], results[1:4], results[4:7]
    return (out.T, *[ref.T.reshape(RANK, 1, SHARE_A) for ref in a_next], *b_next)


def solution(mesh):
    state = P(None, "tensor", "group")
    return jax.shard_map(
        shards,
        mesh=mesh,
        in_specs=(P(None, "tensor"), *[state] * 6, P("group", "tensor"), P("group", "tensor"), P(("group", "tensor"), None)),
        out_specs=(P("group", "tensor"), *[state] * 6),
        check_vma=False,
    )
```

```python
import jax
import jax.numpy as jnp
from jax import lax
from jax.experimental import pallas as pl
from jax.experimental.pallas import tpu as pltpu
from jax.sharding import PartitionSpec as P

beta_one = 0.9
beta_two = 0.999
learn_rate = 0.001
adam_eps = 1e-08
adapter_scale = 2.0
fix_one = 0.9999734386011124
fix_two = 0.0952078528862904

MESH = pl.DeviceIdType.MESH
BF = jnp.bfloat16
F32 = jnp.float32

D, HID, TOK, COLS, ROWS = 5120, 1600, 512, 320, 32
SHARE_A, SHARE_B, RANK = 40, 200, 64
NT, NG = 16, 8

TENSOR_STEPS = sorted(
    ((dx, dy, dc) for dx in range(2) for dy in range(4) for dc in range(2) if (dx, dy, dc) != (0, 0, 0)),
    key=lambda s: -(s[0] + min(s[1], 4 - s[1]) + 0.1 * s[2]),
)
GROUP_STEPS = sorted(
    ((dz, dx) for dz in range(4) for dx in range(2) if (dz, dx) != (0, 0)),
    key=lambda s: -(min(s[0], 4 - s[0]) + 2 * s[1]),
)


def dot(left, right, left_dim, right_dim):
    return lax.dot_general(
        left, right, (((left_dim,), (right_dim,)), ((), ())), preferred_element_type=F32
    )


def aligned(index, size):
    return pl.ds(pl.multiple_of(index * size, size), size)


def kernel(
    base_hbm, ma_hbm, m1a_hbm, m2a_hbm, mb_hbm, m1b_hbm, m2b_hbm, xt_hbm, cot_hbm, xr_hbm,
    acc, b_left, b_right, xa, a_state, b_state,
    base, xt, cot, xall, a_in, b_in, pad, msg0, got0, msg0b, mom_a, mom_b,
    old_a, old_b, part, got1, low, own2, grad_b, grad_a, msg3a, got3a, msg3b, got3b, msg4, got4, b_rows, rows_b,
    a_left, a_right, cross, window_x, part5, got5, own5,
    loc, s0, r0, s0b, r0b, s1, r1, s2, r2, s3a, r3a, s3b, r3b, s4, r4, s5, r5, s6, r6, sx, rx, sc, rc, sw, rw,
):
    g = lax.axis_index("group")
    t = lax.axis_index("tensor")
    z, far = g // 2, lax.rem(g, 2)
    xl, y, core = t // 8, lax.rem(t // 2, 4), lax.rem(t, 2)

    def tensor_at(dx, dy, dc):
        return lax.rem(xl + dx, 2) * 8 + lax.rem(y + dy, 4) * 2 + lax.rem(core + dc, 2)

    def group_at(dz, dx):
        return lax.rem(z + dz, 4) * 2 + lax.rem(far + dx, 2)

    tensor_peers = [tensor_at(*s) for s in TENSOR_STEPS]
    group_peers = [group_at(*s) for s in GROUP_STEPS]

    bar = pltpu.get_barrier_semaphore()
    for gg in group_peers:
        pl.semaphore_signal(bar, inc=1, device_id=(gg, t), device_id_type=MESH)
    for tt in tensor_peers:
        pl.semaphore_signal(bar, inc=1, device_id=(g, tt), device_id_type=MESH)

    def remote(src, dst, ssem, rsem, k, gg, tt):
        copy = pltpu.make_async_remote_copy(
            src_ref=src, dst_ref=dst, send_sem=ssem.at[k], recv_sem=rsem.at[k],
            device_id=(gg, tt), device_id_type=MESH,
        )
        copy.start()
        return copy

    def load(src, dst, k):
        copy = pltpu.make_async_copy(src, dst, loc.at[k])
        copy.start()
        return copy

    load_b = load(mb_hbm, b_in.at[0], 0)
    load_a = load(ma_hbm, a_in.at[0], 1)

    def slot(at_y, dx, dy):
        place = lax.rem(at_y + (2 if (dx, dy) == (1, 0) or (dx, dy) == (0, 2) else 0) + dy, 4)
        late = (dx, dy) == (0, 2) or (dx == 1 and dy != 0)
        return (8 if late else 0) + place * 2

    def rows_of(dx, dy, at_core=core, at_y=y):
        return aligned(slot(at_y, dx, dy) + at_core, ROWS)

    mine = rows_of(0, 0)
    load_x = load(xr_hbm, xall.at[mine], 2)
    load_cot = load(cot_hbm, cot, 3)
    load_xt = load(xt_hbm, xt, 4)
    loads_m = [
        load(m1b_hbm, b_in.at[1], 5), load(m2b_hbm, b_in.at[2], 6),
        load(m1a_hbm, a_in.at[1], 7), load(m2a_hbm, a_in.at[2], 8),
    ]
    load_base = load(base_hbm, base, 9)

    pad[...] = jnp.zeros_like(pad)
    msg0[...] = jnp.zeros_like(msg0)
    load_a.wait()
    pad[0, 0:SHARE_A, 0:RANK] = a_in[0]
    factor_a = pad[0].T[0:RANK, 0:SHARE_A]
    msg0[:, SHARE_B:SHARE_B + SHARE_A] = factor_a.astype(BF)
    load_b.wait()
    msg0[:, 0:SHARE_B] = b_in[0, :, 0, :].astype(BF)
    pl.semaphore_wait(bar, len(group_peers) + len(tensor_peers))
    copies0 = [remote(msg0, got0.at[g], s0, r0, k, gg, t) for k, gg in enumerate(group_peers)]
    got0[g] = msg0[...]

    x_next, y_up, y_down, sibling = tensor_at(1, 0, 0), tensor_at(0, 1, 0), tensor_at(0, 3, 0), tensor_at(0, 0, 1)
    half, quarter = D // 2, D // 4
    own_half, other_half = xl, 1 - xl
    sent_x, sent_share = [], []

    def columns_of(first, count=1):
        return pl.ds(pl.multiple_of(first * quarter, quarter), count * quarter)

    def half_of(i):
        return pl.ds(pl.multiple_of(i * half, half), half)

    def send_x(here, there, at_y, columns, to):
        copy = remote(
            xall.at[rows_of(*here), columns], xall.at[rows_of(*there, at_y=at_y), columns],
            sx, rx, len(sent_x), g, to,
        )
        sent_x.append(copy)
        return copy

    def share_x(here, columns):
        where = xall.at[rows_of(*here), columns]
        copy = remote(where, where, sc, rc, len(sent_share), g, sibling)
        sent_share.append(copy)
        return copy

    def arrived(copies):
        for copy in copies:
            copy.wait_recv()

    everything = pl.ds(0, D)

    def base_part(part, columns):
        tokens = xall[part * 256:(part + 1) * 256, columns]
        for rows in (pl.ds(0, 800), pl.ds(800, 800)):
            acc[part, rows, :] += dot(base[rows, columns], tokens, 1, 1)

    def window_of(tt):
        return pl.ds(pl.multiple_of((tt // 2) * 640 + lax.rem(tt, 2) * 256, 128), 384)

    load_x.wait()
    step_a = [
        send_x((0, 0), (0, 3), y + 1, half_of(own_half), y_up),
        send_x((0, 0), (0, 1), y + 3, half_of(own_half), y_down),
        send_x((0, 0), (1, 0), y, half_of(other_half), x_next),
        send_x((0, 0), (0, 3), y + 1, columns_of(2 * other_half), y_up),
        send_x((0, 0), (0, 1), y + 3, columns_of(2 * other_half + 1), y_down),
    ]
    near = [share_x((0, 0), everything)]

    lanes = lax.broadcasted_iota(jnp.int32, (160, 128), 1)
    left = lanes < RANK

    def beside(first, second):
        rows = first.shape[0]
        return jnp.where(left[0:rows], first, pltpu.roll(second, RANK, 1))

    for copy in loads_m:
        copy.wait()
    for i in range(3):
        pad[1, 0:RANK, 0:128] = b_in[i, :, 0, 0:128]
        pad[2, 0:RANK, 0:SHARE_B - 128] = b_in[i, :, 0, 128:SHARE_B]
        rows_b[0:128, :] = pad[1].T
        rows_b[128:256, :] = pad[2].T
        mom_b[i] = beside(rows_b[0:112, :], rows_b[104:216, :])
    a_left[...] = jnp.zeros_like(a_left)
    a_right[...] = jnp.zeros_like(a_right)
    acc[...] = jnp.zeros_like(acc)
    grad_b[HID:HID + 16, :] = jnp.zeros((16, 128), F32)
    msg0b[...] = jnp.zeros_like(msg0b)
    msg0b[0, :, 0:RANK] = a_in[1]
    msg0b[0, :, RANK:2 * RANK] = a_in[0]
    msg0b[1, :, RANK:2 * RANK] = a_in[2]
    rows_a = aligned(g, SHARE_A)
    mom_a[:, rows_a, :] = msg0b[...]

    for copy in copies0:
        copy.wait_recv()
    for j in range(NG):
        old_b[:, j * SHARE_B:(j + 1) * SHARE_B] = got0[j, :, 0:SHARE_B]
        old_a[:, j * SHARE_A:(j + 1) * SHARE_A] = got0[j, :, SHARE_B:SHARE_B + SHARE_A]
    load_cot.wait()
    load_xt.wait()
    hidden = dot(old_a[...], xt[...], 1, 0)
    back = dot(old_b[...], cot[...], 1, 0)
    for h in range(2):
        part[h, 0:RANK, :] = hidden[:, h * 256:(h + 1) * 256].astype(BF)
        part[h, RANK:, :] = back[:, h * 256:(h + 1) * 256].astype(BF)
    copies1 = [
        remote(part.at[lax.rem(tt, 2), aligned(tt // 2, 16)], got1.at[k], s1, r1, k, g, tt)
        for k, tt in enumerate(tensor_peers)
    ]

    step_b = [
        send_x((0, 0), (0, 3), y + 1, columns_of(2 * other_half + 1), y_up),
        send_x((0, 0), (0, 1), y + 3, columns_of(2 * other_half), y_down),
        send_x((0, 0), (1, 0), y, half_of(own_half), x_next),
    ]

    partner = group_at(0, 1)
    z_peers = [group_at(dz, 0) for dz in (2, 1, 3)]
    copies0b = [
        remote(msg0b, mom_a.at[:, rows_a, :], s0b, r0b, k, gg, t) for k, gg in enumerate([partner] + z_peers)
    ]

    for copy in copies1:
        copy.wait_recv()
    my_half, my_rows = lax.rem(t, 2), aligned(t // 2, 16)
    total = part[my_half, my_rows, :].astype(F32)
    for k in range(NT - 1):
        total = total + got1[k].astype(F32)
    own2[...] = total.astype(BF)
    copies2 = [
        remote(own2, low.at[my_half, my_rows], s2, r2, k, g, tt) for k, tt in enumerate(tensor_peers)
    ]
    low[my_half, my_rows, :] = own2[...]

    arrived(step_a)
    early = []
    for dy in (2, 1, 3):
        for dc in range(2):
            to = tensor_at(0, dy, dc)
            k = 2 * (dy - 1) + dc
            early.append(
                remote(xall.at[rows_of(1, 0), window_of(to)], cross.at[k], sw, rw, k, g, to)
            )
    step_c = [
        send_x((0, 3), (0, 2), y + 1, columns_of(2 * own_half), y_up),
        send_x((0, 1), (0, 2), y + 3, columns_of(2 * own_half + 1), y_down),
        send_x((0, 3), (0, 2), y + 1, columns_of(2 * other_half), y_up),
        send_x((0, 1), (0, 2), y + 3, columns_of(2 * other_half + 1), y_down),
    ]
    step_d = [
        send_x((1, 0), (1, 3), y + 1, half_of(own_half), y_up),
        send_x((1, 0), (1, 1), y + 3, half_of(own_half), y_down),
    ]
    step_e = [
        send_x((0, 1), (1, 1), y, columns_of(2 * own_half + 1), x_next),
        send_x((0, 3), (1, 3), y, columns_of(2 * own_half), x_next),
    ]
    near += [share_x(there, half_of(own_half)) for there in ((1, 0), (0, 1), (0, 3))]
    arrived(step_b)
    near_b = [share_x(there, half_of(other_half)) for there in ((1, 0), (0, 1), (0, 3))]
    step_d += [
        send_x((1, 0), (1, 3), y + 1, columns_of(2 * other_half + 1), y_up),
        send_x((1, 0), (1, 1), y + 3, columns_of(2 * other_half), y_down),
    ]
    copies0b[0].wait_recv()
    rows_partner = aligned(partner, SHARE_A)
    copies0b += [
        remote(mom_a.at[:, rows_partner, :], mom_a.at[:, rows_partner, :], s0b, r0b, 4 + k, gg, t)
        for k, gg in enumerate(z_peers)
    ]

    for copy in copies2:
        copy.wait_recv()

    low0, low1 = low[0], low[1]
    grad_a[...] = dot(xt[:, 0:256], low0, 1, 1) + dot(xt[:, 256:512], low1, 1, 1)
    msg3a[...] = jnp.where(left, pltpu.roll(grad_a[0:160, :], RANK, 1), grad_a[160:320, :]).astype(BF)
    copies3a = [remote(msg3a, got3a.at[g], s3a, r3a, k, gg, t) for k, gg in enumerate(group_peers)]
    got3a[g] = msg3a[...]

    def grad_rows(i, carry):
        rows = aligned(i, 400)
        grad_b[rows, :] = dot(cot[rows, 0:256], low0, 1, 1) + dot(cot[rows, 256:512], low1, 1, 1)
        return carry

    lax.fori_loop(0, HID // 400, grad_rows, 0)

    def message3(j):
        return beside(
            grad_b[pl.ds(pl.multiple_of(j * SHARE_B, 8), 112), :],
            grad_b[pl.ds(pl.multiple_of(j * SHARE_B + 104, 8), 112), :],
        ).astype(BF)

    copies3b = []
    for k, gg in enumerate(group_peers):
        msg3b[k] = message3(gg)
        copies3b.append(remote(msg3b.at[k], got3b.at[g], s3b, r3b, k, gg, t))
    got3b[g] = message3(g)

    arrived(copies0b[1:])

    def packed_right(rows):
        return jnp.where(left, pltpu.roll(rows[0:160], RANK, 1), rows[160:320])

    master_a = packed_right(mom_a[0])
    second_a = packed_right(mom_a[1])
    first_a = beside(mom_a[0, 0:160, :], mom_a[0, 160:320, :])

    load_base.wait()
    arrived(near)
    base_part(0, half_of(own_half))

    arrived(step_c)
    two_away = share_x((0, 2), everything)
    step_f = [send_x((0, 2), (1, 2), y, columns_of(2 * other_half), x_next)]
    arrived(early + [two_away])
    own_window = window_of(t)
    for dx in range(2):
        for dy in range(4):
            for dc in range(2):
                rows = aligned(tensor_at(dx, dy, dc), ROWS)
                held = rows_of(dx, dy, lax.rem(core + dc, 2))
                window_x[rows, :] = cross[2 * ((4 - dy) - 1) + dc] if dx == 1 and dy else xall[held, own_window]

    def adam(master, first, second, got):
        grad = got[0].astype(F32)
        for j in range(1, NG):
            grad = grad + got[j].astype(F32)
        grad = adapter_scale * grad
        first_next = beta_one * first + (1.0 - beta_one) * grad
        second_next = beta_two * second + (1.0 - beta_two) * grad * grad
        master_next = master - learn_rate * (first_next / fix_one) / (
            jnp.sqrt(second_next / fix_two) + adam_eps
        )
        return master_next, first_next, second_next

    for copy in copies3a:
        copy.wait_recv()
    next_a = adam(master_a, first_a, second_a, got3a)
    new_a = next_a[0].astype(BF).astype(F32)
    turned = pltpu.roll(new_a, RANK, 1)
    place = pl.multiple_of(core * RANK, RANK)
    a_left[pl.ds(place, 160), :] = jnp.where(left, new_a, 0.0).astype(BF)
    a_left[pl.ds(place + 160, 160), :] = jnp.where(left, turned, 0.0).astype(BF)
    a_right[pl.ds(place, 160), :] = jnp.where(left, 0.0, turned).astype(BF)
    a_right[pl.ds(place + 160, 160), :] = jnp.where(left, 0.0, new_a).astype(BF)

    part5[...] = (
        dot(window_x[0:256, :], a_left[...], 1, 0) + dot(window_x[256:512, :], a_right[...], 1, 0)
    ).astype(BF)
    copies5 = [
        remote(part5.at[aligned(tt, 16)], got5.at[k], s5, r5, k, g, tt)
        for k, tt in enumerate(tensor_peers)
    ]

    arrived(step_e)
    step_g = [
        send_x((0, 2), (1, 2), y, columns_of(2 * other_half + 1), x_next),
        send_x((1, 1), (1, 2), y + 3, columns_of(2 * other_half + 1), y_down),
        send_x((1, 3), (1, 2), y + 1, columns_of(2 * other_half), y_up),
    ]

    for copy in copies3b:
        copy.wait_recv()
    next_b = adam(mom_b[0], mom_b[1], mom_b[2], got3b)
    msg4[...] = next_b[0].astype(BF)
    copies4 = [remote(msg4, got4.at[g], s4, r4, k, gg, t) for k, gg in enumerate(group_peers)]
    got4[g] = msg4[...]

    arrived(step_d + step_f)
    away_a = [
        share_x((1, 2), columns_of(2 * own_half)),
        share_x((1, 1), everything),
        share_x((1, 3), everything),
    ]
    arrived(near_b)
    base_part(0, half_of(other_half))
    for copy in copies5:
        copy.wait_recv()
    mine5 = aligned(t, 16)
    total = part5[mine5, :].astype(F32)
    for k in range(NT - 1):
        total = total + got5[k].astype(F32)
    own5[...] = (adapter_scale * total).astype(BF)
    copies6 = [remote(own5, xa.at[mine5], s6, r6, k, g, tt) for k, tt in enumerate(tensor_peers)]
    xa[mine5, :] = own5[...]

    arrived(step_g)
    away_b = [share_x((1, 2), columns_of(2 * own_half + 1)), share_x((1, 2), half_of(other_half))]

    rows_out = aligned(lax.rem(g, 4), SHARE_A)
    for i in range(3):
        grad_a[0:160, :] = next_a[i]
        own_rows = grad_a[rows_out, :]
        own_rows = jnp.where(g < 4, own_rows, pltpu.roll(own_rows, RANK, 1))
        a_state[i] = own_rows[:, 0:RANK]
        rows_b[0:104, :] = next_b[i][0:104]
        rows_b[104:200, :] = pltpu.roll(next_b[i], RANK, 1)[0:96]
        b_state[i, :, 0, 0:128] = rows_b[0:128, :].T[0:RANK]
        b_state[i, :, 0, 128:SHARE_B] = rows_b[128:256, :].T[0:RANK, 0:SHARE_B - 128]

    for copy in copies4:
        copy.wait_recv()
    for j in range(NG):
        rows = got4[j].astype(F32)
        b_rows[j * SHARE_B:j * SHARE_B + 104, :] = jnp.where(left[0:104], rows[0:104], 0.0)
        b_rows[j * SHARE_B + 104:(j + 1) * SHARE_B, :] = jnp.where(
            left[0:96], pltpu.roll(rows, RANK, 1)[0:96], 0.0
        )
    b_left[...] = b_rows[...].astype(BF)
    b_right[...] = pltpu.roll(b_rows[...], RANK, 1).astype(BF)

    arrived(away_a + away_b)
    base_part(1, half_of(own_half))
    base_part(1, half_of(other_half))
    for copy in copies6:
        copy.wait_recv()
    for group in (
        copies0, sent_x, sent_share, early, copies0b, copies1, copies2, copies3a, copies3b, copies4, copies5, copies6,
    ):
        for copy in group:
            copy.wait_send()


def finish(
    acc, b_left, b_right, xa, a_state, b_state,
    out_hbm, ma_out, m1a_out, m2a_out, mb_out, m1b_out, m2b_out,
    out_v, sem,
):
    def store(src, dst, k):
        copy = pltpu.make_async_copy(src, dst, sem.at[k])
        copy.start()
        return copy

    t = lax.axis_index("tensor")
    xl, y = t // 8, lax.rem(t // 2, 4)
    place = lax.broadcasted_iota(jnp.int32, (320, 256), 1) // 64
    from_late, from_early = place == lax.rem(y + 2, 4), place == y
    stores = []
    for i in range(5):
        rows = pl.ds(320 * i, 320)
        near, away = acc[0, rows, :], acc[1, rows, :]
        own = jnp.where(from_late, jnp.concatenate([away[:, 128:], away[:, :128]], axis=1), near)
        other = jnp.where(from_early, jnp.concatenate([near[:, 128:], near[:, :128]], axis=1), away)
        out_v[rows, 0:256] = (jnp.where(xl == 0, own, other) + dot(b_left[rows, :], xa[...], 1, 1)).astype(BF)
        out_v[rows, 256:512] = (jnp.where(xl == 0, other, own) + dot(b_right[rows, :], xa[...], 1, 1)).astype(BF)
        stores.append(store(out_v.at[rows], out_hbm.at[rows], i))
        if i == 0:
            stores += [store(a_state.at[j], ref, 5 + j) for j, ref in enumerate((ma_out, m1a_out, m2a_out))]
            stores += [store(b_state.at[j], ref, 8 + j) for j, ref in enumerate((mb_out, m1b_out, m2b_out))]
    for copy in stores:
        copy.wait()


def shards(
    frozen_base_matrix, master_a, moment1_a, moment2_a, master_b, moment1_b, moment2_b,
    learner_token_inputs, learner_output_cotangents, rollout_inputs,
):
    state_a = [ref.reshape(RANK, SHARE_A).T for ref in (master_a, moment1_a, moment2_a)]
    dma = pltpu.SemaphoreType.DMA
    vmem = pltpu.VMEM
    any_space = pl.BlockSpec(memory_space=pl.ANY)
    in_vmem = pl.BlockSpec(memory_space=pltpu.VMEM)
    shape = jax.ShapeDtypeStruct
    mib = 1024 * 1024
    operands = (
        frozen_base_matrix.T, *state_a, master_b, moment1_b, moment2_b,
        learner_token_inputs.T, learner_output_cotangents.T, rollout_inputs,
    )
    parts = pl.pallas_call(
        kernel,
        out_shape=[
            vmem((2, HID, 256), F32),
            vmem((HID, 128), BF),
            vmem((HID, 128), BF),
            vmem((256, 128), BF),
            vmem((3, SHARE_A, RANK), F32),
            vmem((3, RANK, 1, SHARE_B), F32),
        ],
        in_specs=[any_space] * 10,
        out_specs=[in_vmem] * 6,
        scratch_shapes=[
            vmem((HID, D), BF),
            vmem((COLS, TOK), BF),
            vmem((HID, TOK), BF),
            vmem((TOK, D), BF),
            vmem((3, SHARE_A, RANK), F32),
            vmem((3, RANK, 1, SHARE_B), F32),
            vmem((3, 128, 128), F32),
            vmem((RANK, 256), BF),
            vmem((NG, RANK, 256), BF),
            vmem((2, SHARE_A, 128), F32),
            vmem((2, COLS, 128), F32),
            vmem((3, 112, 128), F32),
            vmem((RANK, COLS), BF),
            vmem((RANK, HID), BF),
            vmem((2, 128, 256), BF),
            vmem((NT - 1, 16, 256), BF),
            vmem((2, 128, 256), BF),
            vmem((16, 256), BF),
            vmem((HID + 16, 128), F32),
            vmem((COLS, 128), F32),
            vmem((160, 128), BF),
            vmem((NG, 160, 128), BF),
            vmem((NG - 1, 112, 128), BF),
            vmem((NG, 112, 128), BF),
            vmem((112, 128), BF),
            vmem((NG, 112, 128), BF),
            vmem((HID, 128), F32),
            vmem((256, 128), F32),
            vmem((384, 128), BF),
            vmem((384, 128), BF),
            vmem((6, ROWS, 384), BF),
            vmem((TOK, 384), BF),
            vmem((256, 128), BF),
            vmem((NT - 1, 16, 128), BF),
            vmem((16, 128), BF),
            dma((10,)),
        ]
        + [dma((n,)) for n in (7, 7, 7, 7, 15, 15, 15, 15, 7, 7, 7, 7, 7, 7, 15, 15, 15, 15, 22, 22, 13, 13, 6, 6)],
        compiler_params=pltpu.CompilerParams(
            collective_id=0, has_side_effects=True, vmem_limit_bytes=44 * mib
        ),
        cost_estimate=pl.CostEstimate(
            flops=2 * TOK * D * HID, bytes_accessed=2 * (D * HID + 2 * TOK * HID), transcendentals=0
        ),
    )(*[pltpu.with_memory_space_constraint(operand, pltpu.HBM) for operand in operands])
    results = pl.pallas_call(
        finish,
        out_shape=[shape((HID, TOK), BF)]
        + [shape((SHARE_A, RANK), F32)] * 3
        + [shape((RANK, 1, SHARE_B), F32)] * 3,
        in_specs=[in_vmem] * 6,
        out_specs=[any_space] * 7,
        scratch_shapes=[vmem((HID, TOK), BF), dma((11,))],
        compiler_params=pltpu.CompilerParams(vmem_limit_bytes=10 * mib),
        cost_estimate=pl.CostEstimate(
            flops=2 * TOK * RANK * HID, bytes_accessed=2 * TOK * HID, transcendentals=0
        ),
    )(*parts)
    out, a_next, b_next = results[0], results[1:4], results[4:7]
    return (out.T, *[ref.T.reshape(RANK, 1, SHARE_A) for ref in a_next], *b_next)


def solution(mesh):
    state = P(None, "tensor", "group")
    return jax.shard_map(
        shards,
        mesh=mesh,
        in_specs=(P(None, "tensor"), *[state] * 6, P("group", "tensor"), P("group", "tensor"), P(("group", "tensor"), None)),
        out_specs=(P("group", "tensor"), *[state] * 6),
        check_vma=False,
    )
```

```python
import jax
import jax.numpy as jnp
from jax import lax
from jax.experimental import pallas as pl
from jax.experimental.pallas import tpu as pltpu
from jax.sharding import PartitionSpec as P

beta_one = 0.9
beta_two = 0.999
learn_rate = 0.001
adam_eps = 1e-08
adapter_scale = 2.0
fix_one = 0.9999734386011124
fix_two = 0.0952078528862904

MESH = pl.DeviceIdType.MESH
BF = jnp.bfloat16
F32 = jnp.float32

D, HID, TOK, COLS, ROWS = 5120, 1600, 512, 320, 32
SHARE_A, SHARE_B, RANK = 40, 200, 64
NT, NG = 16, 8

TENSOR_STEPS = sorted(
    ((dx, dy, dc) for dx in range(2) for dy in range(4) for dc in range(2) if (dx, dy, dc) != (0, 0, 0)),
    key=lambda s: -(s[0] + min(s[1], 4 - s[1]) + 0.1 * s[2]),
)
GROUP_STEPS = sorted(
    ((dz, dx) for dz in range(4) for dx in range(2) if (dz, dx) != (0, 0)),
    key=lambda s: -(min(s[0], 4 - s[0]) + 2 * s[1]),
)


def dot(left, right, left_dim, right_dim):
    return lax.dot_general(
        left, right, (((left_dim,), (right_dim,)), ((), ())), preferred_element_type=F32
    )


def aligned(index, size):
    return pl.ds(pl.multiple_of(index * size, size), size)


def kernel(
    base_hbm, ma_hbm, m1a_hbm, m2a_hbm, mb_hbm, m1b_hbm, m2b_hbm, xt_hbm, cot_hbm, xr_hbm,
    acc, b_left, b_right, xa, a_state, b_state,
    base, xt, cot, xall, a_in, b_in, pad, msg0, got0, msg0b, mom_a, mom_b,
    old_a, old_b, part, got1, low, own2, grad_b, grad_a, msg3a, got3a, msg3b, got3b, msg4, got4, b_rows, rows_b,
    a_left, a_right, cross, window_x, part5, got5, own5,
    loc, s0, r0, s0b, r0b, s1, r1, s2, r2, s3a, r3a, s3b, r3b, s4, r4, s5, r5, s6, r6, sx, rx, sc, rc, sw, rw,
):
    g = lax.axis_index("group")
    t = lax.axis_index("tensor")
    z, far = g // 2, lax.rem(g, 2)
    xl, y, core = t // 8, lax.rem(t // 2, 4), lax.rem(t, 2)

    def tensor_at(dx, dy, dc):
        return lax.rem(xl + dx, 2) * 8 + lax.rem(y + dy, 4) * 2 + lax.rem(core + dc, 2)

    def group_at(dz, dx):
        return lax.rem(z + dz, 4) * 2 + lax.rem(far + dx, 2)

    tensor_peers = [tensor_at(*s) for s in TENSOR_STEPS]
    group_peers = [group_at(*s) for s in GROUP_STEPS]

    bar = pltpu.get_barrier_semaphore()
    for gg in group_peers:
        pl.semaphore_signal(bar, inc=1, device_id=(gg, t), device_id_type=MESH)
    for tt in tensor_peers:
        pl.semaphore_signal(bar, inc=1, device_id=(g, tt), device_id_type=MESH)

    def remote(src, dst, ssem, rsem, k, gg, tt):
        copy = pltpu.make_async_remote_copy(
            src_ref=src, dst_ref=dst, send_sem=ssem.at[k], recv_sem=rsem.at[k],
            device_id=(gg, tt), device_id_type=MESH,
        )
        copy.start()
        return copy

    def load(src, dst, k):
        copy = pltpu.make_async_copy(src, dst, loc.at[k])
        copy.start()
        return copy

    load_b = load(mb_hbm, b_in.at[0], 0)
    load_a = load(ma_hbm, a_in.at[0], 1)

    def slot(at_y, dx, dy):
        place = lax.rem(at_y + (2 if (dx, dy) == (1, 0) or (dx, dy) == (0, 2) else 0) + dy, 4)
        late = (dx, dy) == (0, 2) or (dx == 1 and dy != 0)
        return (8 if late else 0) + place * 2

    def rows_of(dx, dy, at_core=core, at_y=y):
        return aligned(slot(at_y, dx, dy) + at_core, ROWS)

    mine = rows_of(0, 0)
    load_x = load(xr_hbm, xall.at[mine], 2)
    load_cot = load(cot_hbm, cot, 3)
    load_xt = load(xt_hbm, xt, 4)
    loads_m = [
        load(m1b_hbm, b_in.at[1], 5), load(m2b_hbm, b_in.at[2], 6),
        load(m1a_hbm, a_in.at[1], 7), load(m2a_hbm, a_in.at[2], 8),
    ]
    load_base = load(base_hbm, base, 9)

    pad[...] = jnp.zeros_like(pad)
    msg0[...] = jnp.zeros_like(msg0)
    load_a.wait()
    pad[0, 0:SHARE_A, 0:RANK] = a_in[0]
    factor_a = pad[0].T[0:RANK, 0:SHARE_A]
    msg0[:, SHARE_B:SHARE_B + SHARE_A] = factor_a.astype(BF)
    load_b.wait()
    msg0[:, 0:SHARE_B] = b_in[0, :, 0, :].astype(BF)
    pl.semaphore_wait(bar, len(group_peers) + len(tensor_peers))
    copies0 = [remote(msg0, got0.at[g], s0, r0, k, gg, t) for k, gg in enumerate(group_peers)]
    got0[g] = msg0[...]

    x_next, y_up, y_down, sibling = tensor_at(1, 0, 0), tensor_at(0, 1, 0), tensor_at(0, 3, 0), tensor_at(0, 0, 1)
    half, quarter = D // 2, D // 4
    own_half, other_half = xl, 1 - xl
    sent_x, sent_share = [], []

    def columns_of(first, count=1):
        return pl.ds(pl.multiple_of(first * quarter, quarter), count * quarter)

    def half_of(i):
        return pl.ds(pl.multiple_of(i * half, half), half)

    def send_x(here, there, at_y, columns, to):
        copy = remote(
            xall.at[rows_of(*here), columns], xall.at[rows_of(*there, at_y=at_y), columns],
            sx, rx, len(sent_x), g, to,
        )
        sent_x.append(copy)
        return copy

    def share_x(here, columns):
        where = xall.at[rows_of(*here), columns]
        copy = remote(where, where, sc, rc, len(sent_share), g, sibling)
        sent_share.append(copy)
        return copy

    def arrived(copies):
        for copy in copies:
            copy.wait_recv()

    everything = pl.ds(0, D)

    def base_part(part, columns):
        tokens = xall[part * 256:(part + 1) * 256, columns]
        for rows in (pl.ds(0, 800), pl.ds(800, 800)):
            acc[part, rows, :] += dot(base[rows, columns], tokens, 1, 1)

    def window_of(tt):
        return pl.ds(pl.multiple_of((tt // 2) * 640 + lax.rem(tt, 2) * 256, 128), 384)

    load_x.wait()
    step_a = [
        send_x((0, 0), (0, 3), y + 1, half_of(own_half), y_up),
        send_x((0, 0), (0, 1), y + 3, half_of(own_half), y_down),
        send_x((0, 0), (1, 0), y, half_of(other_half), x_next),
        send_x((0, 0), (0, 3), y + 1, columns_of(2 * other_half), y_up),
        send_x((0, 0), (0, 1), y + 3, columns_of(2 * other_half + 1), y_down),
    ]
    near = [share_x((0, 0), everything)]

    lanes = lax.broadcasted_iota(jnp.int32, (160, 128), 1)
    left = lanes < RANK

    def beside(first, second):
        rows = first.shape[0]
        return jnp.where(left[0:rows], first, pltpu.roll(second, RANK, 1))

    for copy in loads_m:
        copy.wait()
    for i in range(3):
        pad[1, 0:RANK, 0:128] = b_in[i, :, 0, 0:128]
        pad[2, 0:RANK, 0:SHARE_B - 128] = b_in[i, :, 0, 128:SHARE_B]
        rows_b[0:128, :] = pad[1].T
        rows_b[128:256, :] = pad[2].T
        mom_b[i] = beside(rows_b[0:112, :], rows_b[104:216, :])
    a_left[...] = jnp.zeros_like(a_left)
    a_right[...] = jnp.zeros_like(a_right)
    acc[...] = jnp.zeros_like(acc)
    grad_b[HID:HID + 16, :] = jnp.zeros((16, 128), F32)
    msg0b[...] = jnp.zeros_like(msg0b)
    msg0b[0, :, 0:RANK] = a_in[1]
    msg0b[0, :, RANK:2 * RANK] = a_in[0]
    msg0b[1, :, RANK:2 * RANK] = a_in[2]
    rows_a = aligned(g, SHARE_A)
    mom_a[:, rows_a, :] = msg0b[...]

    for copy in copies0:
        copy.wait_recv()
    for j in range(NG):
        old_b[:, j * SHARE_B:(j + 1) * SHARE_B] = got0[j, :, 0:SHARE_B]
        old_a[:, j * SHARE_A:(j + 1) * SHARE_A] = got0[j, :, SHARE_B:SHARE_B + SHARE_A]
    load_cot.wait()
    load_xt.wait()
    hidden = dot(old_a[...], xt[...], 1, 0)
    back = dot(old_b[...], cot[...], 1, 0)
    for h in range(2):
        part[h, 0:RANK, :] = hidden[:, h * 256:(h + 1) * 256].astype(BF)
        part[h, RANK:, :] = back[:, h * 256:(h + 1) * 256].astype(BF)
    copies1 = [
        remote(part.at[lax.rem(tt, 2), aligned(tt // 2, 16)], got1.at[k], s1, r1, k, g, tt)
        for k, tt in enumerate(tensor_peers)
    ]

    step_b = [
        send_x((0, 0), (0, 3), y + 1, columns_of(2 * other_half + 1), y_up),
        send_x((0, 0), (0, 1), y + 3, columns_of(2 * other_half), y_down),
        send_x((0, 0), (1, 0), y, half_of(own_half), x_next),
    ]

    partner = group_at(0, 1)
    z_peers = [group_at(dz, 0) for dz in (2, 1, 3)]
    copies0b = [
        remote(msg0b, mom_a.at[:, rows_a, :], s0b, r0b, k, gg, t) for k, gg in enumerate([partner] + z_peers)
    ]

    for copy in copies1:
        copy.wait_recv()
    my_half, my_rows = lax.rem(t, 2), aligned(t // 2, 16)
    total = part[my_half, my_rows, :].astype(F32)
    for k in range(NT - 1):
        total = total + got1[k].astype(F32)
    own2[...] = total.astype(BF)
    copies2 = [
        remote(own2, low.at[my_half, my_rows], s2, r2, k, g, tt) for k, tt in enumerate(tensor_peers)
    ]
    low[my_half, my_rows, :] = own2[...]

    arrived(step_a)
    early = []
    for dy in (2, 1, 3):
        for dc in range(2):
            to = tensor_at(0, dy, dc)
            k = 2 * (dy - 1) + dc
            early.append(
                remote(xall.at[rows_of(1, 0), window_of(to)], cross.at[k], sw, rw, k, g, to)
            )
    step_c = [
        send_x((0, 3), (0, 2), y + 1, columns_of(2 * own_half), y_up),
        send_x((0, 1), (0, 2), y + 3, columns_of(2 * own_half + 1), y_down),
        send_x((0, 3), (0, 2), y + 1, columns_of(2 * other_half), y_up),
        send_x((0, 1), (0, 2), y + 3, columns_of(2 * other_half + 1), y_down),
    ]
    step_d = [
        send_x((1, 0), (1, 3), y + 1, half_of(own_half), y_up),
        send_x((1, 0), (1, 1), y + 3, half_of(own_half), y_down),
    ]
    step_e = [
        send_x((0, 1), (1, 1), y, columns_of(2 * own_half + 1), x_next),
        send_x((0, 3), (1, 3), y, columns_of(2 * own_half), x_next),
    ]
    near += [share_x(there, half_of(own_half)) for there in ((1, 0), (0, 1), (0, 3))]
    arrived(step_b)
    near_b = [share_x(there, half_of(other_half)) for there in ((1, 0), (0, 1), (0, 3))]
    step_d += [
        send_x((1, 0), (1, 3), y + 1, columns_of(2 * other_half + 1), y_up),
        send_x((1, 0), (1, 1), y + 3, columns_of(2 * other_half), y_down),
    ]
    copies0b[0].wait_recv()
    rows_partner = aligned(partner, SHARE_A)
    copies0b += [
        remote(mom_a.at[:, rows_partner, :], mom_a.at[:, rows_partner, :], s0b, r0b, 4 + k, gg, t)
        for k, gg in enumerate(z_peers)
    ]

    for copy in copies2:
        copy.wait_recv()

    low0, low1 = low[0], low[1]
    grad_a[...] = dot(xt[:, 0:256], low0, 1, 1) + dot(xt[:, 256:512], low1, 1, 1)
    msg3a[...] = jnp.where(left, pltpu.roll(grad_a[0:160, :], RANK, 1), grad_a[160:320, :]).astype(BF)
    copies3a = [remote(msg3a, got3a.at[g], s3a, r3a, k, gg, t) for k, gg in enumerate(group_peers)]
    got3a[g] = msg3a[...]

    def grad_rows(i, carry):
        rows = aligned(i, 400)
        grad_b[rows, :] = dot(cot[rows, 0:256], low0, 1, 1) + dot(cot[rows, 256:512], low1, 1, 1)
        return carry

    lax.fori_loop(0, HID // 400, grad_rows, 0)

    def message3(j):
        return beside(
            grad_b[pl.ds(pl.multiple_of(j * SHARE_B, 8), 112), :],
            grad_b[pl.ds(pl.multiple_of(j * SHARE_B + 104, 8), 112), :],
        ).astype(BF)

    copies3b = []
    for k, gg in enumerate(group_peers):
        msg3b[k] = message3(gg)
        copies3b.append(remote(msg3b.at[k], got3b.at[g], s3b, r3b, k, gg, t))
    got3b[g] = message3(g)

    arrived(copies0b[1:])

    def packed_right(rows):
        return jnp.where(left, pltpu.roll(rows[0:160], RANK, 1), rows[160:320])

    master_a = packed_right(mom_a[0])
    second_a = packed_right(mom_a[1])
    first_a = beside(mom_a[0, 0:160, :], mom_a[0, 160:320, :])

    load_base.wait()
    arrived(near)
    base_part(0, half_of(own_half))

    arrived(step_c)
    two_away = share_x((0, 2), everything)
    step_f = [send_x((0, 2), (1, 2), y, columns_of(2 * other_half), x_next)]
    arrived(step_e)
    step_g = [
        send_x((0, 2), (1, 2), y, columns_of(2 * other_half + 1), x_next),
        send_x((1, 1), (1, 2), y + 3, columns_of(2 * other_half + 1), y_down),
        send_x((1, 3), (1, 2), y + 1, columns_of(2 * other_half), y_up),
    ]

    arrived(near_b)
    base_part(0, half_of(other_half))

    arrived(early + [two_away])
    own_window = window_of(t)
    for dx in range(2):
        for dy in range(4):
            for dc in range(2):
                rows = aligned(tensor_at(dx, dy, dc), ROWS)
                held = rows_of(dx, dy, lax.rem(core + dc, 2))
                window_x[rows, :] = cross[2 * ((4 - dy) - 1) + dc] if dx == 1 and dy else xall[held, own_window]

    def adam(master, first, second, got):
        grad = got[0].astype(F32)
        for j in range(1, NG):
            grad = grad + got[j].astype(F32)
        grad = adapter_scale * grad
        first_next = beta_one * first + (1.0 - beta_one) * grad
        second_next = beta_two * second + (1.0 - beta_two) * grad * grad
        master_next = master - learn_rate * (first_next / fix_one) / (
            jnp.sqrt(second_next / fix_two) + adam_eps
        )
        return master_next, first_next, second_next

    for copy in copies3a:
        copy.wait_recv()
    next_a = adam(master_a, first_a, second_a, got3a)
    new_a = next_a[0].astype(BF).astype(F32)
    turned = pltpu.roll(new_a, RANK, 1)
    place = pl.multiple_of(core * RANK, RANK)
    a_left[pl.ds(place, 160), :] = jnp.where(left, new_a, 0.0).astype(BF)
    a_left[pl.ds(place + 160, 160), :] = jnp.where(left, turned, 0.0).astype(BF)
    a_right[pl.ds(place, 160), :] = jnp.where(left, 0.0, turned).astype(BF)
    a_right[pl.ds(place + 160, 160), :] = jnp.where(left, 0.0, new_a).astype(BF)

    part5[...] = (
        dot(window_x[0:256, :], a_left[...], 1, 0) + dot(window_x[256:512, :], a_right[...], 1, 0)
    ).astype(BF)
    copies5 = [
        remote(part5.at[aligned(tt, 16)], got5.at[k], s5, r5, k, g, tt)
        for k, tt in enumerate(tensor_peers)
    ]

    for copy in copies3b:
        copy.wait_recv()
    next_b = adam(mom_b[0], mom_b[1], mom_b[2], got3b)
    msg4[...] = next_b[0].astype(BF)
    copies4 = [remote(msg4, got4.at[g], s4, r4, k, gg, t) for k, gg in enumerate(group_peers)]
    got4[g] = msg4[...]

    arrived(step_d + step_f)
    away_a = [
        share_x((1, 2), columns_of(2 * own_half)),
        share_x((1, 1), everything),
        share_x((1, 3), everything),
    ]

    rows_out = aligned(lax.rem(g, 4), SHARE_A)
    for i in range(3):
        grad_a[0:160, :] = next_a[i]
        own_rows = grad_a[rows_out, :]
        own_rows = jnp.where(g < 4, own_rows, pltpu.roll(own_rows, RANK, 1))
        a_state[i] = own_rows[:, 0:RANK]
        rows_b[0:104, :] = next_b[i][0:104]
        rows_b[104:200, :] = pltpu.roll(next_b[i], RANK, 1)[0:96]
        b_state[i, :, 0, 0:128] = rows_b[0:128, :].T[0:RANK]
        b_state[i, :, 0, 128:SHARE_B] = rows_b[128:256, :].T[0:RANK, 0:SHARE_B - 128]

    arrived(step_g)
    away_b = [share_x((1, 2), columns_of(2 * own_half + 1)), share_x((1, 2), half_of(other_half))]
    arrived(away_a + away_b[:1])
    base_part(1, half_of(own_half))

    for copy in copies5:
        copy.wait_recv()
    mine5 = aligned(t, 16)
    total = part5[mine5, :].astype(F32)
    for k in range(NT - 1):
        total = total + got5[k].astype(F32)
    own5[...] = (adapter_scale * total).astype(BF)
    copies6 = [remote(own5, xa.at[mine5], s6, r6, k, g, tt) for k, tt in enumerate(tensor_peers)]
    xa[mine5, :] = own5[...]

    for copy in copies4:
        copy.wait_recv()
    for j in range(NG):
        rows = got4[j].astype(F32)
        b_rows[j * SHARE_B:j * SHARE_B + 104, :] = jnp.where(left[0:104], rows[0:104], 0.0)
        b_rows[j * SHARE_B + 104:(j + 1) * SHARE_B, :] = jnp.where(
            left[0:96], pltpu.roll(rows, RANK, 1)[0:96], 0.0
        )
    b_left[...] = b_rows[...].astype(BF)
    b_right[...] = pltpu.roll(b_rows[...], RANK, 1).astype(BF)

    arrived(away_b[1:])
    base_part(1, half_of(other_half))
    for copy in copies6:
        copy.wait_recv()
    for group in (
        copies0, sent_x, sent_share, early, copies0b, copies1, copies2, copies3a, copies3b, copies4, copies5, copies6,
    ):
        for copy in group:
            copy.wait_send()


def finish(
    acc, b_left, b_right, xa, a_state, b_state,
    out_hbm, ma_out, m1a_out, m2a_out, mb_out, m1b_out, m2b_out,
    out_v, sem,
):
    def store(src, dst, k):
        copy = pltpu.make_async_copy(src, dst, sem.at[k])
        copy.start()
        return copy

    t = lax.axis_index("tensor")
    xl, y = t // 8, lax.rem(t // 2, 4)
    place = lax.broadcasted_iota(jnp.int32, (320, 256), 1) // 64
    from_late, from_early = place == lax.rem(y + 2, 4), place == y
    stores = []
    for i in range(5):
        rows = pl.ds(320 * i, 320)
        near, away = acc[0, rows, :], acc[1, rows, :]
        own = jnp.where(from_late, jnp.concatenate([away[:, 128:], away[:, :128]], axis=1), near)
        other = jnp.where(from_early, jnp.concatenate([near[:, 128:], near[:, :128]], axis=1), away)
        out_v[rows, 0:256] = (jnp.where(xl == 0, own, other) + dot(b_left[rows, :], xa[...], 1, 1)).astype(BF)
        out_v[rows, 256:512] = (jnp.where(xl == 0, other, own) + dot(b_right[rows, :], xa[...], 1, 1)).astype(BF)
        stores.append(store(out_v.at[rows], out_hbm.at[rows], i))
        if i == 0:
            stores += [store(a_state.at[j], ref, 5 + j) for j, ref in enumerate((ma_out, m1a_out, m2a_out))]
            stores += [store(b_state.at[j], ref, 8 + j) for j, ref in enumerate((mb_out, m1b_out, m2b_out))]
    for copy in stores:
        copy.wait()


def shards(
    frozen_base_matrix, master_a, moment1_a, moment2_a, master_b, moment1_b, moment2_b,
    learner_token_inputs, learner_output_cotangents, rollout_inputs,
):
    state_a = [ref.reshape(RANK, SHARE_A).T for ref in (master_a, moment1_a, moment2_a)]
    dma = pltpu.SemaphoreType.DMA
    vmem = pltpu.VMEM
    any_space = pl.BlockSpec(memory_space=pl.ANY)
    in_vmem = pl.BlockSpec(memory_space=pltpu.VMEM)
    shape = jax.ShapeDtypeStruct
    mib = 1024 * 1024
    operands = (
        frozen_base_matrix.T, *state_a, master_b, moment1_b, moment2_b,
        learner_token_inputs.T, learner_output_cotangents.T, rollout_inputs,
    )
    parts = pl.pallas_call(
        kernel,
        out_shape=[
            vmem((2, HID, 256), F32),
            vmem((HID, 128), BF),
            vmem((HID, 128), BF),
            vmem((256, 128), BF),
            vmem((3, SHARE_A, RANK), F32),
            vmem((3, RANK, 1, SHARE_B), F32),
        ],
        in_specs=[any_space] * 10,
        out_specs=[in_vmem] * 6,
        scratch_shapes=[
            vmem((HID, D), BF),
            vmem((COLS, TOK), BF),
            vmem((HID, TOK), BF),
            vmem((TOK, D), BF),
            vmem((3, SHARE_A, RANK), F32),
            vmem((3, RANK, 1, SHARE_B), F32),
            vmem((3, 128, 128), F32),
            vmem((RANK, 256), BF),
            vmem((NG, RANK, 256), BF),
            vmem((2, SHARE_A, 128), F32),
            vmem((2, COLS, 128), F32),
            vmem((3, 112, 128), F32),
            vmem((RANK, COLS), BF),
            vmem((RANK, HID), BF),
            vmem((2, 128, 256), BF),
            vmem((NT - 1, 16, 256), BF),
            vmem((2, 128, 256), BF),
            vmem((16, 256), BF),
            vmem((HID + 16, 128), F32),
            vmem((COLS, 128), F32),
            vmem((160, 128), BF),
            vmem((NG, 160, 128), BF),
            vmem((NG - 1, 112, 128), BF),
            vmem((NG, 112, 128), BF),
            vmem((112, 128), BF),
            vmem((NG, 112, 128), BF),
            vmem((HID, 128), F32),
            vmem((256, 128), F32),
            vmem((384, 128), BF),
            vmem((384, 128), BF),
            vmem((6, ROWS, 384), BF),
            vmem((TOK, 384), BF),
            vmem((256, 128), BF),
            vmem((NT - 1, 16, 128), BF),
            vmem((16, 128), BF),
            dma((10,)),
        ]
        + [dma((n,)) for n in (7, 7, 7, 7, 15, 15, 15, 15, 7, 7, 7, 7, 7, 7, 15, 15, 15, 15, 22, 22, 13, 13, 6, 6)],
        compiler_params=pltpu.CompilerParams(
            collective_id=0, has_side_effects=True, vmem_limit_bytes=44 * mib
        ),
        cost_estimate=pl.CostEstimate(
            flops=2 * TOK * D * HID, bytes_accessed=2 * (D * HID + 2 * TOK * HID), transcendentals=0
        ),
    )(*[pltpu.with_memory_space_constraint(operand, pltpu.HBM) for operand in operands])
    results = pl.pallas_call(
        finish,
        out_shape=[shape((HID, TOK), BF)]
        + [shape((SHARE_A, RANK), F32)] * 3
        + [shape((RANK, 1, SHARE_B), F32)] * 3,
        in_specs=[in_vmem] * 6,
        out_specs=[any_space] * 7,
        scratch_shapes=[vmem((HID, TOK), BF), dma((11,))],
        compiler_params=pltpu.CompilerParams(vmem_limit_bytes=10 * mib),
        cost_estimate=pl.CostEstimate(
            flops=2 * TOK * RANK * HID, bytes_accessed=2 * TOK * HID, transcendentals=0
        ),
    )(*parts)
    out, a_next, b_next = results[0], results[1:4], results[4:7]
    return (out.T, *[ref.T.reshape(RANK, 1, SHARE_A) for ref in a_next], *b_next)


def solution(mesh):
    state = P(None, "tensor", "group")
    return jax.shard_map(
        shards,
        mesh=mesh,
        in_specs=(P(None, "tensor"), *[state] * 6, P("group", "tensor"), P("group", "tensor"), P(("group", "tensor"), None)),
        out_specs=(P("group", "tensor"), *[state] * 6),
        check_vma=False,
    )
```
